128 devices in a mesh: dp: 128 (over y, x, z, core).
Axes of the slice: x: 4, y: 4, z: 4, core: 2. Of those that a mesh axis runs over, the one named last changes fastest.
Arguments:
- queries: bfloat16 [65536, 4096], P('dp'), may hold values from -16 to 16
- passages: bfloat16 [65536, 4096], P('dp'), may hold values from -16 to 16
- links: int32 [128, 3], P('dp'), may hold values 0 or 1
- positives: int32 [128, 512], P('dp'), may hold values from 0 to 511, each once within a row
Outputs:
- query_grad: bfloat16 [65536, 4096], P('dp')
- passage_grad: bfloat16 [65536, 4096], P('dp')
- row_loss: float32 [65536], P('dp')
- col_loss: float32 [65536], P('dp')
The draws below stay inside these ranges and needn't reach their ends.
All inputs are finite; a program needn't handle non-finite values. No bound on the sum of `links` on one device may be relied on, other than what follows from the above.
Results may differ from the reference program's by a relative error of at most 0.0048.
Values may be sent and summed in bfloat16 or wider, within the bound.
A program may use at most 192 MiB of HBM per device.

```python
import jax
import jax.numpy as jnp
from jax import lax

D = 4096
B = 512
HOPS = 3
NBLK = 128
ROWS = 65536
N_DP = 128


def draw_queries(key, part):
    key = jax.random.fold_in(key, 5)
    values = jnp.clip(jax.random.normal(key, (ROWS, D), jnp.float32), -6.0, 6.0)
    return values.astype(jnp.bfloat16)


def draw_passages(key, part):
    key = jax.random.fold_in(key, 7)
    values = jnp.clip(jax.random.normal(key, (ROWS, D), jnp.float32), -6.0, 6.0)
    return values.astype(jnp.bfloat16)


def with_ends(values, key, smallest, high):
    index_at = [jax.random.randint(jax.random.fold_in(key, axis), (), 0, length) for axis, length in enumerate(values.shape)]
    widest = values.shape.index(max(values.shape))
    neighbour = index_at[:widest] + [(index_at[widest] + 1) % values.shape[widest]] + index_at[widest + 1:]
    return values.at[tuple(index_at)].set(smallest).at[tuple(neighbour)].set(high)


def setup_inputs(seed: int = 0) -> dict:
    keys = jax.random.split(jax.random.key(seed), 5)
    queries = draw_queries(jax.random.fold_in(keys[4], 71), 0)
    passages = draw_passages(jax.random.fold_in(keys[4], 71), 0)
    links = with_ends((jax.random.randint(keys[2], (NBLK, HOPS), 0, 2) < 1).astype(jnp.int32), jax.random.fold_in(keys[2], 1), 0, 1)
    positives = jax.vmap(lambda own: jax.random.permutation(own, B))(jax.random.split(keys[3], NBLK)).reshape((NBLK, B)).astype(jnp.int32)
    return dict(queries=queries, passages=passages, links=links, positives=positives)


def reference(queries, passages, links, positives):
    factor = D ** -0.5
    query_blocks = queries.astype(jnp.float32).reshape(N_DP, B, D)
    passage_blocks = passages.astype(jnp.float32).reshape(N_DP, B, D)
    live = jnp.concatenate([jnp.ones((N_DP, 1), jnp.int32), links], axis=1) > 0
    tiles = []
    for offset in range(HOPS + 1):
        shifted = jnp.roll(passage_blocks, -offset, axis=0)
        tile = jnp.einsum("brd,bcd->brc", query_blocks, shifted) * factor
        tiles.append(jnp.where(live[:, offset, None, None], tile, -jnp.inf))
    stacked = jnp.stack(tiles)
    row_max = jnp.max(stacked, axis=(0, 3))
    row_lse = row_max + jnp.log(jnp.sum(jnp.exp(stacked - row_max[None, :, :, None]), axis=(0, 3)))
    col_maxima = jnp.stack([jnp.roll(jnp.max(tiles[offset], axis=1), offset, axis=0) for offset in range(HOPS + 1)])
    col_top = jnp.max(col_maxima, axis=0)
    col_sum = jnp.zeros((N_DP, B), jnp.float32)
    for offset in range(HOPS + 1):
        partial_sum = jnp.sum(jnp.exp(tiles[offset] - jnp.roll(col_top, -offset, axis=0)[:, None, :]), axis=1)
        col_sum = col_sum + jnp.roll(partial_sum, offset, axis=0)
    col_lse = col_top + jnp.log(col_sum)
    matches = (positives[:, :, None] == jnp.arange(B, dtype=jnp.int32)[None, None, :]).astype(jnp.float32)
    query_grad = jnp.zeros((N_DP, B, D), jnp.float32)
    passage_grad = jnp.zeros((N_DP, B, D), jnp.float32)
    for offset in range(HOPS + 1):
        tile = tiles[offset]
        weights = jnp.exp(tile - row_lse[:, :, None]) + jnp.exp(tile - jnp.roll(col_lse, -offset, axis=0)[:, None, :])
        if offset == 0:
            weights = weights - 2.0 * matches
        weights = lax.optimization_barrier(weights.astype(jnp.bfloat16)).astype(jnp.float32)
        shifted = jnp.roll(passage_blocks, -offset, axis=0)
        query_grad = query_grad + jnp.einsum("brc,bcd->brd", weights, shifted) * factor
        term = jnp.einsum("brc,brd->bcd", weights, query_blocks) * factor
        if offset > 0:
            term = lax.optimization_barrier(term.astype(jnp.bfloat16)).astype(jnp.float32)
        passage_grad = passage_grad + jnp.roll(term, offset, axis=0)
    row_positive = jnp.sum(matches * tiles[0], axis=2)
    col_positive = jnp.sum(matches * tiles[0], axis=1)
    return (query_grad.reshape(ROWS, D).astype(jnp.bfloat16),
            passage_grad.reshape(ROWS, D).astype(jnp.bfloat16),
            (row_lse - row_positive).reshape(ROWS),
            (col_lse - col_positive).reshape(ROWS))
```

```python
import functools

import jax
import jax.numpy as jnp
from jax import lax
from jax.experimental import pallas as pl
from jax.experimental.pallas import tpu as pltpu
from jax.sharding import PartitionSpec as P

MESH = pl.DeviceIdType.MESH
NEG = -1e30
PIECES = 4
STRIP = 64


def kernel(
    n,
    q_hbm,
    p_hbm,
    links_ref,
    pos_ref,
    dq_hbm,
    dp_hbm,
    row_ref,
    col_ref,
    own,
    far,
    score,
    weight,
    lse,
    stage,
    matches,
    said,
    heard,
    flag_out,
    flag_in,
    load_sem,
    send_sem,
    recv_sem,
    said_sem,
    heard_sem,
    flag_send_sem,
    flag_recv_sem,
    stage_sem,
):
    block, depth = q_hbm.shape
    factor = depth ** (-0.5)
    rows = block // PIECES
    me = lax.axis_index("dp")
    second = lax.rem(me, 2)

    def at(offset):
        return (lax.rem(me + offset + n, n),)

    barrier = pltpu.get_barrier_semaphore()
    for offset in (1, 2, 3, -1, -2, -3):
        pl.semaphore_signal(barrier, inc=1, device_id=at(offset), device_id_type=MESH)
    pl.semaphore_wait(barrier, 6)

    def piece(s):
        return pl.ds(pl.multiple_of(s * rows, rows), rows)

    def send(stream, s, src, slot, offset):
        return pltpu.make_async_remote_copy(
            src_ref=src.at[piece(s)],
            dst_ref=far.at[slot, piece(s)],
            send_sem=send_sem.at[stream, s],
            recv_sem=recv_sem.at[slot, s],
            device_id=at(offset),
            device_id_type=MESH,
        )

    def q_up(s):
        return send(0, s, q_hbm, 4, 2)

    def p_down(s):
        return send(1, s, p_hbm, 1, -2)

    def p_on(s):
        return send(2, s, far.at[1], 2, -1)

    def q_on(s):
        return send(3, s, far.at[4], 5, 1)

    def first_own(s):
        return send(4, s, q_hbm, 3, 1)

    def first_on(s):
        return send(5, s, far.at[1], 0, 1)

    def second_own(s):
        return send(4, s, p_hbm, 0, -1)

    def second_on(s):
        return send(5, s, far.at[4], 3, -1)

    def arrived(slot, s):
        send(0, s, q_hbm, slot, 1).wait_recv()

    def over_pieces(body):
        def step(s, carry):
            body(s)
            return carry

        lax.fori_loop(0, PIECES, step, 0)

    @pl.when(second == 0)
    def _():
        over_pieces(lambda s: p_down(s).start())
        over_pieces(lambda s: first_own(s).start())
        over_pieces(lambda s: q_up(s).start())

    @pl.when(second == 1)
    def _():
        over_pieces(lambda s: q_up(s).start())
        over_pieces(lambda s: p_down(s).start())
        over_pieces(lambda s: second_own(s).start())

    load_q = pltpu.make_async_copy(q_hbm, own.at[0], load_sem.at[0])
    load_p = pltpu.make_async_copy(p_hbm, own.at[1], load_sem.at[1])
    load_q.start()
    load_p.start()

    for k in range(3):
        flag_out[k] = jnp.full((8, 128), links_ref[0, k].astype(jnp.float32), jnp.float32)

    def flag_copy(k):
        return pltpu.make_async_remote_copy(
            src_ref=flag_out.at[k],
            dst_ref=flag_in.at[k],
            send_sem=flag_send_sem.at[k],
            recv_sem=flag_recv_sem.at[k],
            device_id=at(k + 1),
            device_id_type=MESH,
        )

    for k in range(3):
        flag_copy(k).start()

    pos = pos_ref[...].astype(jnp.float32)
    down = lax.broadcasted_iota(jnp.int32, (block, block), 0).astype(jnp.float32)
    matches[1] = (pos == down).astype(jnp.float32)
    upright = jnp.transpose(jnp.broadcast_to(pos, (128, block)))[:, 0:1]
    across = lax.broadcasted_iota(jnp.int32, (block, block), 1).astype(jnp.float32)
    matches[0] = (upright == across).astype(jnp.float32)

    load_q.wait()
    load_p.wait()

    def dot_t(a, b):
        return lax.dot_general(a, b, (((1,), (1,)), ((), ())), preferred_element_type=jnp.float32)

    def diagonal(t, carry):
        side, s = t // PIECES, lax.rem(t, PIECES)
        score[side * 4, :, piece(s)] = dot_t(own[side], own[1 - side, piece(s), :]) * factor
        return carry

    lax.fori_loop(0, 2 * PIECES, diagonal, 0)
    for k in range(3):
        flag_copy(k).wait()

    def score_piece(side, k, s):
        part = dot_t(own[side], far[side * 3 + k - 1, piece(s), :]) * factor
        mine = flag_out[k - 1, 0:1, :]
        theirs = flag_in[k - 1, 0:1, :]
        live = jnp.where(side == 0, mine, theirs)[:, 0:1]
        score[side * 4 + k, :, piece(s)] = jnp.where(live > 0, part, NEG)

    def near(s):
        arrived(1, s)
        p_on(s).start()

        @pl.when(second == 0)
        def _():
            first_on(s).start()

        arrived(4, s)
        q_on(s).start()

        @pl.when(second == 1)
        def _():
            second_on(s).start()

        arrived(0, s)
        arrived(3, s)

        def one(t, carry):
            score_piece(t // 2, lax.rem(t, 2) + 1, s)
            return carry

        lax.fori_loop(0, 4, one, 0)

    over_pieces(near)

    def last(s):
        arrived(2, s)
        arrived(5, s)

        def one(side, carry):
            score_piece(side, 3, s)
            return carry

        lax.fori_loop(0, 2, one, 0)

    over_pieces(last)

    strips = block // STRIP

    def strip(i):
        return pl.ds(pl.multiple_of(i * STRIP, STRIP), STRIP)

    def finish_lse(t, carry):
        side, i = t // strips, lax.rem(t, strips)
        tiles = [score[side * 4 + k, strip(i), :] for k in range(4)]
        top = functools.reduce(jnp.maximum, tiles)
        top = jnp.max(top, axis=1, keepdims=True)
        total = functools.reduce(jnp.add, [jnp.exp(tile - top) for tile in tiles])
        total = jnp.sum(total, axis=1, keepdims=True)
        lse[side, strip(i), :] = jnp.broadcast_to(top + jnp.log(total), (STRIP, 128))
        return carry

    lax.fori_loop(0, 2 * strips, finish_lse, 0)

    def tell(side, k):
        return pltpu.make_async_remote_copy(
            src_ref=said.at[side],
            dst_ref=heard.at[(1 - side) * 3 + k - 1],
            send_sem=said_sem.at[side * 3 + k - 1],
            recv_sem=heard_sem.at[(1 - side) * 3 + k - 1],
            device_id=at(k if side == 0 else -k),
            device_id_type=MESH,
        )

    for side in range(2):
        said[side] = jnp.transpose(lse[side])[0:8, :]
        for k in (1, 2, 3):
            tell(side, k).start()

    row_ref[...] = said[0, 0:1, :] - jnp.sum(matches[1] * score[4], axis=0, keepdims=True)
    col_ref[...] = said[1, 0:1, :] - jnp.sum(matches[0] * score[0], axis=0, keepdims=True)

    def weigh(side, k, i):
        tile = score[side * 4 + k, strip(i), :]
        theirs = said[1 - side, 0:1, :] if k == 0 else heard[side * 3 + k - 1, 0:1, :]
        value = jnp.exp(tile - lse[side, strip(i), 0:1]) + jnp.exp(tile - theirs)
        if k == 0:
            value = value - 2.0 * matches[side, strip(i), :]
        weight[side * 4 + k, strip(i), :] = value.astype(jnp.bfloat16)

    def weigh_diagonal(t, carry):
        weigh(0, 0, t)
        weigh(1, 0, t)
        return carry

    lax.fori_loop(0, strips, weigh_diagonal, 0)
    for side in range(2):
        for k in (1, 2, 3):
            tell(side, k).wait_send()
            tell(side, k).wait_recv()

    def weigh_far(t, carry):
        for side in range(2):
            for k in (1, 2, 3):
                weigh(side, k, t)
        return carry

    lax.fori_loop(0, strips, weigh_far, 0)

    width = stage.shape[2]
    parts = depth // width

    def out_copy(side, j):
        hbm = dq_hbm if side == 0 else dp_hbm
        return pltpu.make_async_copy(
            stage.at[lax.rem(j, 2)],
            hbm.at[:, pl.ds(pl.multiple_of(j * width, width), width)],
            stage_sem.at[lax.rem(j, 2)],
        )

    for side in range(2):

        def grad(j, carry):
            columns = pl.ds(pl.multiple_of(j * width, width), width)
            total = jnp.dot(
                weight[side * 4], own[1 - side, :, columns], preferred_element_type=jnp.float32
            )
            for k in (1, 2, 3):
                total += jnp.dot(
                    weight[side * 4 + k],
                    far[side * 3 + k - 1, :, columns],
                    preferred_element_type=jnp.float32,
                )

            @pl.when(j >= 2)
            def _():
                out_copy(side, j - 2).wait()

            stage[lax.rem(j, 2)] = (total * factor).astype(jnp.bfloat16)
            out_copy(side, j).start()
            return carry

        lax.fori_loop(0, parts, grad, 0)
        out_copy(side, parts - 2).wait()
        out_copy(side, parts - 1).wait()

    over_pieces(lambda s: q_up(s).wait_send())
    over_pieces(lambda s: p_down(s).wait_send())
    over_pieces(lambda s: p_on(s).wait_send())
    over_pieces(lambda s: q_on(s).wait_send())

    @pl.when(second == 0)
    def _():
        over_pieces(lambda s: first_own(s).wait_send())
        over_pieces(lambda s: first_on(s).wait_send())

    @pl.when(second == 1)
    def _():
        over_pieces(lambda s: second_own(s).wait_send())
        over_pieces(lambda s: second_on(s).wait_send())


def local(n, queries, passages, links, positives):
    block, depth = queries.shape
    width = min(512, depth // 2)
    flops = 16 * 2 * block * block * depth
    query_grad, passage_grad, row_loss, col_loss = pl.pallas_call(
        functools.partial(kernel, n),
        out_shape=(
            jax.ShapeDtypeStruct((block, depth), jnp.bfloat16),
            jax.ShapeDtypeStruct((block, depth), jnp.bfloat16),
            jax.ShapeDtypeStruct((1, block), jnp.float32),
            jax.ShapeDtypeStruct((1, block), jnp.float32),
        ),
        in_specs=[
            pl.BlockSpec(memory_space=pl.ANY),
            pl.BlockSpec(memory_space=pl.ANY),
            pl.BlockSpec(memory_space=pltpu.SMEM),
            pl.BlockSpec(memory_space=pltpu.VMEM),
        ],
        out_specs=(
            pl.BlockSpec(memory_space=pl.ANY),
            pl.BlockSpec(memory_space=pl.ANY),
            pl.BlockSpec(memory_space=pltpu.VMEM),
            pl.BlockSpec(memory_space=pltpu.VMEM),
        ),
        scratch_shapes=[
            pltpu.VMEM((2, block, depth), jnp.bfloat16),
            pltpu.VMEM((6, block, depth), jnp.bfloat16),
            pltpu.VMEM((8, block, block), jnp.float32),
            pltpu.VMEM((8, block, block), jnp.bfloat16),
            pltpu.VMEM((2, block, 128), jnp.float32),
            pltpu.VMEM((2, block, width), jnp.bfloat16),
            pltpu.VMEM((2, block, block), jnp.float32),
            pltpu.VMEM((2, 8, block), jnp.float32),
            pltpu.VMEM((6, 8, block), jnp.float32),
            pltpu.VMEM((3, 8, 128), jnp.float32),
            pltpu.VMEM((3, 8, 128), jnp.float32),
            pltpu.SemaphoreType.DMA((2,)),
            pltpu.SemaphoreType.DMA((6, PIECES)),
            pltpu.SemaphoreType.DMA((6, PIECES)),
            pltpu.SemaphoreType.DMA((6,)),
            pltpu.SemaphoreType.DMA((6,)),
            pltpu.SemaphoreType.DMA((3,)),
            pltpu.SemaphoreType.DMA((3,)),
            pltpu.SemaphoreType.DMA((2,)),
        ],
        cost_estimate=pl.CostEstimate(
            flops=flops, bytes_accessed=8 * block * depth, transcendentals=24 * block * block
        ),
        compiler_params=pltpu.CompilerParams(
            collective_id=0, has_side_effects=True, vmem_limit_bytes=60 * 1024 * 1024
        ),
    )(queries, passages, links, positives)
    return query_grad, passage_grad, row_loss.reshape(block), col_loss.reshape(block)


def solution(mesh):
    placed = (P("dp", None), P("dp", None), P("dp", None), P("dp", None))
    return jax.shard_map(
        functools.partial(local, mesh.size),
        mesh=mesh,
        in_specs=placed,
        out_specs=(P("dp", None), P("dp", None), P("dp"), P("dp")),
        check_vma=False,
    )
```

```python
import functools

import jax
import jax.numpy as jnp
from jax import lax
from jax.experimental import pallas as pl
from jax.experimental.pallas import tpu as pltpu
from jax.sharding import PartitionSpec as P

MESH = pl.DeviceIdType.MESH
NEG = -1e30
PIECES = 4
STRIP = 64


def kernel(
    n,
    q_hbm,
    p_hbm,
    links_ref,
    pos_ref,
    dq_hbm,
    dp_hbm,
    row_ref,
    col_ref,
    own,
    far,
    acc,
    weight,
    top,
    mass,
    lse,
    stage,
    upright,
    hit,
    said,
    heard,
    extra,
    stat_out,
    stat_in,
    flag_out,
    flag_in,
    load_sem,
    send_sem,
    recv_sem,
    said_sem,
    heard_sem,
    flag_send_sem,
    flag_recv_sem,
    stat_send_sem,
    stat_recv_sem,
    stage_sem,
):
    block, depth = q_hbm.shape
    factor = depth ** (-0.5)
    rows = block // PIECES
    me = lax.axis_index("dp")
    second = lax.rem(me, 2)
    is_first = second == 0
    is_second = second == 1
    late = (2, 4 + second)

    def at(offset):
        return (lax.rem(me + offset + n, n),)

    barrier = pltpu.get_barrier_semaphore()
    for offset in (1, 2, 3, 4, -1, -2, -3, -4):
        pl.semaphore_signal(barrier, inc=1, device_id=at(offset), device_id_type=MESH)
    pl.semaphore_wait(barrier, 8)

    def piece(s):
        return pl.ds(pl.multiple_of(s * rows, rows), rows)

    def send(stream, s, src, slot, offset):
        return pltpu.make_async_remote_copy(
            src_ref=src.at[piece(s)],
            dst_ref=far.at[slot, piece(s)],
            send_sem=send_sem.at[stream, s],
            recv_sem=recv_sem.at[slot, s],
            device_id=at(offset),
            device_id_type=MESH,
        )

    def q_up(s):
        return send(0, s, q_hbm, 4, 2)

    def p_down(s):
        return send(1, s, p_hbm, 1, -2)

    def p_on(s):
        return send(2, s, far.at[1], 2, -1)

    def q_on(s):
        return send(3, s, far.at[4], 5, 1)

    def first_own(s):
        return send(4, s, q_hbm, 3, 1)

    def first_on(s):
        return send(5, s, far.at[1], 0, 1)

    def second_own(s):
        return send(4, s, p_hbm, 0, -1)

    def second_on(s):
        return send(5, s, far.at[4], 3, -1)

    def q_pass(s):
        return send(7, s, far.at[3], 4, 1)

    def p_pass(s):
        return send(6, s, far.at[0], 2, -2)

    def arrived(slot, s):
        send(0, s, q_hbm, slot, 1).wait_recv()

    def loop(count, body):
        def step(s, carry):
            body(s)
            return carry

        lax.fori_loop(0, count, step, 0)

    for k in range(3):
        flag_out[k] = jnp.full((8, 128), links_ref[0, k].astype(jnp.float32), jnp.float32)

    def flag_copy(k):
        return pltpu.make_async_remote_copy(
            src_ref=flag_out.at[k],
            dst_ref=flag_in.at[k],
            send_sem=flag_send_sem.at[k],
            recv_sem=flag_recv_sem.at[k],
            device_id=at(k + 1),
            device_id_type=MESH,
        )

    for k in range(3):
        flag_copy(k).start()

    @pl.when(is_first)
    def _():
        loop(PIECES, lambda s: p_down(s).start())
        loop(PIECES, lambda s: first_own(s).start())

    @pl.when(is_second)
    def _():
        loop(PIECES, lambda s: q_up(s).start())
        loop(PIECES, lambda s: p_down(s).start())
        loop(PIECES, lambda s: second_own(s).start())

    load_q = pltpu.make_async_copy(q_hbm, own.at[0], load_sem.at[0])
    load_p = pltpu.make_async_copy(p_hbm, own.at[1], load_sem.at[1])
    load_q.start()
    load_p.start()

    pos = pos_ref[...].astype(jnp.float32)
    upright[...] = jnp.transpose(jnp.broadcast_to(pos, (128, block)))
    top[...] = jnp.full(top.shape, NEG, jnp.float32)
    mass[...] = jnp.zeros(mass.shape, jnp.float32)

    @pl.when(is_first)
    def _():
        line = lax.broadcasted_iota(jnp.int32, (8, block), 0)
        stat_in[0] = jnp.where(line < 4, NEG, 0.0)

    load_q.wait()
    load_p.wait()

    def dot_t(a, b):
        return lax.dot_general(a, b, (((1,), (1,)), ((), ())), preferred_element_type=jnp.float32)

    def fold(side, part):
        before = top[side]
        now = jnp.maximum(before, part)
        mass[side] = mass[side] * jnp.exp(before - now) + jnp.exp(part - now)
        top[side] = now

    def diagonal(t):
        side, s = t // PIECES, lax.rem(t, PIECES)
        part = dot_t(own[side], own[1 - side, piece(s), :]) * factor
        acc[0, side * 3, :, piece(s)] = part
        fold(side, part)

    loop(2 * PIECES, diagonal)
    down = lax.broadcasted_iota(jnp.int32, (block, block), 0).astype(jnp.float32)
    across = lax.broadcasted_iota(jnp.int32, (block, block), 1).astype(jnp.float32)
    row_hit = jnp.sum(jnp.where(pos == down, acc[0, 3], 0.0), axis=0, keepdims=True)
    hit[0] = jnp.broadcast_to(row_hit, (8, block))
    col_hit = jnp.sum(
        jnp.where(upright[:, 0:1] == across, acc[0, 0], 0.0), axis=0, keepdims=True
    )
    hit[1] = jnp.broadcast_to(col_hit, (8, block))
    for k in range(3):
        flag_copy(k).wait_recv()

    def live(side, part, k):
        flag = (flag_out if side == 0 else flag_in)[k - 1, 0:1, 0:1]
        return jnp.where(flag > 0, part, NEG)

    def scores(side, slot, k, s):
        return live(side, dot_t(own[side], far[slot, piece(s), :]) * factor, k)

    def tell_stats(index, part, s):
        largest = jnp.max(part, axis=0, keepdims=True)
        total = jnp.sum(jnp.exp(part - largest), axis=0, keepdims=True)
        line = lax.broadcasted_iota(jnp.int32, (8, rows), 0)
        stat_out[index, :, piece(s)] = jnp.where(line < 4, largest, total)

    def first_far(s):
        arrived(5, s)
        part = scores(1, 5, 3, s)
        acc[0, 5, :, piece(s)] = part
        fold(1, part)
        tell_stats(2, part, s)

    def near(s):
        arrived(1, s)

        @pl.when(is_first)
        def _():
            first_on(s).start()

        @pl.when(is_second)
        def _():
            p_on(s).start()

        part = scores(0, 1, 2, s)
        acc[0, 2, :, piece(s)] = part
        fold(0, part)

        @pl.when(is_first)
        def _():
            tell_stats(0, part, s)

        @pl.when(is_first)
        def _():
            arrived(3, s)

        part = scores(1, 3, 1, s)
        acc[0, 4, :, piece(s)] = part
        fold(1, part)
        arrived(0, s)

        @pl.when(is_second)
        def _():
            p_pass(s).start()

        part = scores(0, 0, 1, s)
        acc[0, 1, :, piece(s)] = part
        fold(0, part)

        @pl.when(is_first)
        def _():
            arrived(2, s)
            part = scores(0, 2, 3, s)
            fold(0, part)
            tell_stats(1, part, s)

            @pl.when(s >= 1)
            def _():
                first_far(s - 1)

    @pl.when(is_second)
    def _():
        loop(PIECES, lambda s: arrived(3, s))

        def early(u):
            arrived(4, u)
            q_on(u).start()
            second_on(u).start()
            part = scores(1, 4, 2, u)
            acc[0, 5, :, piece(u)] = part
            fold(1, part)

        loop(PIECES, early)
        loop(PIECES, lambda u: q_pass(u).start())

    loop(PIECES, near)

    def stat_copy(index, slot, offset):
        return pltpu.make_async_remote_copy(
            src_ref=stat_out.at[index],
            dst_ref=stat_in.at[slot],
            send_sem=stat_send_sem.at[index],
            recv_sem=stat_recv_sem.at[slot],
            device_id=at(offset),
            device_id_type=MESH,
        )

    stat_copies = (stat_copy(0, 1, 2), stat_copy(1, 1, 3), stat_copy(2, 0, -3))

    @pl.when(is_first)
    def _():
        stat_copies[0].start()
        stat_copies[1].start()
        first_far(PIECES - 1)
        stat_copies[2].start()

    @pl.when(is_second)
    def _():
        stat_copies[2].wait_recv()

    stat_copies[0].wait_recv()

    def tell(index, src, dst, offset):
        return pltpu.make_async_remote_copy(
            src_ref=src,
            dst_ref=extra if dst is None else heard.at[dst],
            send_sem=said_sem.at[index],
            recv_sem=heard_sem.at[6 if dst is None else dst],
            device_id=at(offset),
            device_id_type=MESH,
        )

    def first_tells(side):
        sign = 1 if side == 0 else -1
        return [
            tell(side * 3 + k - 1, said.at[side], (1 - side) * 3 + k - 1, sign * k)
            for k in (1, 2, 3)
        ]

    def passed_tells():
        up = [tell(6 + k, extra, 3 + k, 2 + k) for k in range(3)]
        return up + [tell(8 + k, heard.at[0], k, -k) for k in (1, 2)]

    def second_tells(side):
        return [tell(side, said.at[side], None if side == 0 else 0, -1)]

    for side in range(2):
        tops = jnp.transpose(top[side])
        largest = jnp.max(tops, axis=0, keepdims=True)
        total = jnp.sum(
            jnp.transpose(mass[side]) * jnp.exp(tops - largest), axis=0, keepdims=True
        )
        other = stat_in[side, 0:1, :]
        both = jnp.maximum(largest, other)
        total = total * jnp.exp(largest - both) + stat_in[side, 4:5, :] * jnp.exp(other - both)
        value = both + jnp.log(total)
        said[side] = jnp.broadcast_to(value, (8, block))

        @pl.when(is_first)
        def _():
            for copy in first_tells(side):
                copy.start()

        @pl.when(is_second)
        def _():
            for copy in second_tells(side):
                copy.start()

        lse[side] = jnp.transpose(jnp.broadcast_to(value, (128, block)))

    row_ref[...] = said[0, 0:1, :] - hit[0, 0:1, :]
    col_ref[...] = said[1, 0:1, :] - hit[1, 0:1, :]

    strips = block // STRIP

    def strip(i):
        return pl.ds(pl.multiple_of(i * STRIP, STRIP), STRIP)

    def weigh(side, index, theirs, i):
        tile = acc[0, side * 3 + index, strip(i), :]
        value = jnp.exp(tile - lse[side, strip(i), 0:1]) + jnp.exp(tile - theirs)
        if index == 0:
            if side == 0:
                lanes = lax.broadcasted_iota(jnp.int32, (STRIP, block), 1).astype(jnp.float32)
                match = upright[strip(i), 0:1] == lanes
            else:
                lines = lax.broadcasted_iota(jnp.int32, (STRIP, block), 0) + i * STRIP
                match = pos_ref[...] == lines
            value = value - jnp.where(match, 2.0, 0.0)
        weight[side * 3 + index, strip(i), :] = value.astype(jnp.bfloat16)

    def weigh_diagonal(i):
        for side in range(2):
            weigh(side, 0, said[1 - side, 0:1, :], i)

    def told(dst):
        tell(0, said.at[0], dst, 1).wait_recv()

    told(0)

    @pl.when(is_first)
    def _():
        told(None)
        for copy in passed_tells():
            copy.start()

    loop(strips, weigh_diagonal)
    for dst in range(1, 6):
        told(dst)

    def weigh_far(i):
        weigh(0, 1, heard[0, 0:1, :], i)
        weigh(0, 2, heard[1, 0:1, :], i)
        weigh(1, 1, heard[3, 0:1, :], i)
        weigh(1, 2, heard[5 - second, 0:1, :], i)

    loop(strips, weigh_far)

    width = stage.shape[2]
    parts = depth // width

    def columns(j):
        return pl.ds(pl.multiple_of(j * width, width), width)

    for side in range(2):

        def early_grad(j):
            slots = (0, 1) if side == 0 else (3, 5 - second)
            total = jnp.dot(
                weight[side * 3], own[1 - side, :, columns(j)], preferred_element_type=jnp.float32
            )
            for index, slot in enumerate(slots):
                total += jnp.dot(
                    weight[side * 3 + 1 + index],
                    far[slot, :, columns(j)],
                    preferred_element_type=jnp.float32,
                )
            acc[side, j] = total

        loop(parts, early_grad)

    def weigh_late(side, s):
        slot = late[side]
        k = 3 if side == 0 else 2 + second
        part = scores(side, slot, k, s)
        theirs = heard[slot, 0:1, piece(s)]
        value = jnp.exp(part - lse[side, :, 0:1]) + jnp.exp(part - theirs)
        weight[6 + side, :, piece(s)] = value.astype(jnp.bfloat16)

    def out_copy(side, j):
        hbm = dq_hbm if side == 0 else dp_hbm
        return pltpu.make_async_copy(
            stage.at[lax.rem(j, 2)], hbm.at[:, columns(j)], stage_sem.at[lax.rem(j, 2)]
        )

    def finish(side):
        def late_grad(j):
            total = acc[side, j] + jnp.dot(
                weight[6 + side], far[late[side], :, columns(j)], preferred_element_type=jnp.float32
            )

            @pl.when(j >= 2)
            def _():
                out_copy(side, j - 2).wait()

            stage[lax.rem(j, 2)] = (total * factor).astype(jnp.bfloat16)
            out_copy(side, j).start()

        loop(parts, late_grad)
        out_copy(side, parts - 2).wait()
        out_copy(side, parts - 1).wait()

    def late_piece(s):
        @pl.when(is_second)
        def _():
            arrived(2, s)

        weigh_late(0, s)

        @pl.when(is_first)
        def _():
            arrived(4, s)
            q_on(s).start()

        @pl.when(is_second)
        def _():
            arrived(5, s)

        weigh_late(1, s)

    loop(PIECES, late_piece)
    finish(0)
    finish(1)

    for k in range(3):
        flag_copy(k).wait_send()
    for copy in (p_down, q_on):
        loop(PIECES, lambda s: copy(s).wait_send())

    @pl.when(is_first)
    def _():
        for copy in (first_own, first_on):
            loop(PIECES, lambda s: copy(s).wait_send())
        for copy in stat_copies + tuple(first_tells(0) + first_tells(1) + passed_tells()):
            copy.wait_send()

    @pl.when(is_second)
    def _():
        for copy in (q_up, p_on, second_own, second_on, p_pass, q_pass):
            loop(PIECES, lambda s: copy(s).wait_send())
        for copy in second_tells(0) + second_tells(1):
            copy.wait_send()


def local(n, queries, passages, links, positives):
    block, depth = queries.shape
    width = min(block, depth // 2)
    flops = 16 * 2 * block * block * depth
    query_grad, passage_grad, row_loss, col_loss = pl.pallas_call(
        functools.partial(kernel, n),
        out_shape=(
            jax.ShapeDtypeStruct((block, depth), jnp.bfloat16),
            jax.ShapeDtypeStruct((block, depth), jnp.bfloat16),
            jax.ShapeDtypeStruct((1, block), jnp.float32),
            jax.ShapeDtypeStruct((1, block), jnp.float32),
        ),
        in_specs=[
            pl.BlockSpec(memory_space=pl.ANY),
            pl.BlockSpec(memory_space=pl.ANY),
            pl.BlockSpec(memory_space=pltpu.SMEM),
            pl.BlockSpec(memory_space=pltpu.VMEM),
        ],
        out_specs=(
            pl.BlockSpec(memory_space=pl.ANY),
            pl.BlockSpec(memory_space=pl.ANY),
            pl.BlockSpec(memory_space=pltpu.VMEM),
            pl.BlockSpec(memory_space=pltpu.VMEM),
        ),
        scratch_shapes=[
            pltpu.VMEM((2, block, depth), jnp.bfloat16),
            pltpu.VMEM((6, block, depth), jnp.bfloat16),
            pltpu.VMEM((2, max(depth // width, 6), block, width), jnp.float32),
            pltpu.VMEM((8, block, block), jnp.bfloat16),
            pltpu.VMEM((2, block, 128), jnp.float32),
            pltpu.VMEM((2, block, 128), jnp.float32),
            pltpu.VMEM((2, block, 128), jnp.float32),
            pltpu.VMEM((2, block, width), jnp.bfloat16),
            pltpu.VMEM((block, 128), jnp.float32),
            pltpu.VMEM((2, 8, block), jnp.float32),
            pltpu.VMEM((2, 8, block), jnp.float32),
            pltpu.VMEM((6, 8, block), jnp.float32),
            pltpu.VMEM((8, block), jnp.float32),
            pltpu.VMEM((3, 8, block), jnp.float32),
            pltpu.VMEM((2, 8, block), jnp.float32),
            pltpu.VMEM((3, 8, 128), jnp.float32),
            pltpu.VMEM((3, 8, 128), jnp.float32),
            pltpu.SemaphoreType.DMA((2,)),
            pltpu.SemaphoreType.DMA((8, PIECES)),
            pltpu.SemaphoreType.DMA((6, PIECES)),
            pltpu.SemaphoreType.DMA((11,)),
            pltpu.SemaphoreType.DMA((7,)),
            pltpu.SemaphoreType.DMA((3,)),
            pltpu.SemaphoreType.DMA((3,)),
            pltpu.SemaphoreType.DMA((3,)),
            pltpu.SemaphoreType.DMA((2,)),
            pltpu.SemaphoreType.DMA((2,)),
        ],
        cost_estimate=pl.CostEstimate(
            flops=flops, bytes_accessed=8 * block * depth, transcendentals=24 * block * block
        ),
        compiler_params=pltpu.CompilerParams(
            collective_id=0, has_side_effects=True, vmem_limit_bytes=60 * 1024 * 1024
        ),
    )(queries, passages, links, positives)
    return query_grad, passage_grad, row_loss.reshape(block), col_loss.reshape(block)


def solution(mesh):
    placed = (P("dp", None), P("dp", None), P("dp", None), P("dp", None))
    return jax.shard_map(
        functools.partial(local, mesh.size),
        mesh=mesh,
        in_specs=placed,
        out_specs=(P("dp", None), P("dp", None), P("dp"), P("dp")),
        check_vma=False,
    )
```

```python
import functools

import jax
import jax.numpy as jnp
from jax import lax
from jax.experimental import pallas as pl
from jax.experimental.pallas import tpu as pltpu
from jax.sharding import PartitionSpec as P

MESH = pl.DeviceIdType.MESH
NEG = -1e30
PIECES = 4
STRIP = 64


def kernel(
    n,
    q_hbm,
    p_hbm,
    links_ref,
    pos_ref,
    dq_hbm,
    dp_hbm,
    row_ref,
    col_ref,
    own,
    far,
    acc,
    weight,
    top,
    mass,
    lse,
    stage,
    upright,
    hit,
    said,
    heard,
    extra,
    stat_out,
    stat_in,
    flag_out,
    flag_in,
    load_sem,
    send_sem,
    recv_sem,
    said_sem,
    heard_sem,
    flag_send_sem,
    flag_recv_sem,
    stat_send_sem,
    stat_recv_sem,
    stage_sem,
):
    block, depth = q_hbm.shape
    factor = depth ** (-0.5)
    rows = block // PIECES
    me = lax.axis_index("dp")
    second = lax.rem(me, 2)
    is_first = second == 0
    is_second = second == 1
    late = (2, 4 + second)

    def at(offset):
        return (lax.rem(me + offset + n, n),)

    barrier = pltpu.get_barrier_semaphore()
    for offset in (1, 2, 3, 4, -1, -2, -3, -4):
        pl.semaphore_signal(barrier, inc=1, device_id=at(offset), device_id_type=MESH)
    pl.semaphore_wait(barrier, 8)

    def piece(s):
        return pl.ds(pl.multiple_of(s * rows, rows), rows)

    def send(stream, s, src, slot, offset):
        return pltpu.make_async_remote_copy(
            src_ref=src.at[piece(s)],
            dst_ref=far.at[slot, piece(s)],
            send_sem=send_sem.at[stream, s],
            recv_sem=recv_sem.at[slot, s],
            device_id=at(offset),
            device_id_type=MESH,
        )

    def q_up(s):
        return send(0, s, q_hbm, 4, 2)

    def p_down(s):
        return send(1, s, p_hbm, 1, -2)

    def p_on(s):
        return send(2, s, far.at[1], 2, -1)

    def q_on(s):
        return send(3, s, far.at[4], 5, 1)

    def first_own(s):
        return send(4, s, q_hbm, 3, 1)

    def first_on(s):
        return send(5, s, far.at[1], 0, 1)

    def second_own(s):
        return send(4, s, p_hbm, 0, -1)

    def second_on(s):
        return send(5, s, far.at[4], 3, -1)

    def q_pass(s):
        return send(7, s, far.at[3], 4, 1)

    def p_pass(s):
        return send(6, s, far.at[0], 2, -2)

    def arrived(slot, s):
        send(0, s, q_hbm, slot, 1).wait_recv()

    def loop(count, body):
        def step(s, carry):
            body(s)
            return carry

        lax.fori_loop(0, count, step, 0)

    for k in range(3):
        flag_out[k] = jnp.full((8, 128), links_ref[0, k].astype(jnp.float32), jnp.float32)

    def flag_copy(k):
        return pltpu.make_async_remote_copy(
            src_ref=flag_out.at[k],
            dst_ref=flag_in.at[k],
            send_sem=flag_send_sem.at[k],
            recv_sem=flag_recv_sem.at[k],
            device_id=at(k + 1),
            device_id_type=MESH,
        )

    for k in range(3):
        flag_copy(k).start()

    @pl.when(is_first)
    def _():
        loop(PIECES, lambda s: p_down(s).start())
        loop(PIECES, lambda s: first_own(s).start())

    @pl.when(is_second)
    def _():
        loop(PIECES, lambda s: q_up(s).start())
        loop(PIECES, lambda s: p_down(s).start())
        loop(PIECES, lambda s: second_own(s).start())

    load_q = pltpu.make_async_copy(q_hbm, own.at[0], load_sem.at[0])
    load_p = pltpu.make_async_copy(p_hbm, own.at[1], load_sem.at[1])
    load_q.start()
    load_p.start()

    pos = pos_ref[...].astype(jnp.float32)
    upright[...] = jnp.transpose(jnp.broadcast_to(pos, (128, block)))
    top[...] = jnp.full(top.shape, NEG, jnp.float32)
    mass[...] = jnp.zeros(mass.shape, jnp.float32)

    @pl.when(is_first)
    def _():
        line = lax.broadcasted_iota(jnp.int32, (8, block), 0)
        stat_in[0] = jnp.where(line < 4, NEG, 0.0)

    load_q.wait()
    load_p.wait()

    def dot_t(a, b):
        return lax.dot_general(a, b, (((1,), (1,)), ((), ())), preferred_element_type=jnp.float32)

    def fold(side, part):
        before = top[side]
        now = jnp.maximum(before, part)
        mass[side] = mass[side] * jnp.exp(before - now) + jnp.exp(part - now)
        top[side] = now

    def tile(index, start, size):
        per = stage.shape[2] // block
        first = lax.rem(index, per) * block + start
        return (0, index // per, slice(None), pl.ds(pl.multiple_of(first, 128), size))

    def keep(side, index, part, s):
        acc[tile(index, s * rows, rows)] = part
        fold(side, part)

    def diagonal(t):
        side, s = t // PIECES, lax.rem(t, PIECES)
        keep(side, side * 3, dot_t(own[side], own[1 - side, piece(s), :]) * factor, s)

    loop(2 * PIECES, diagonal)
    down = lax.broadcasted_iota(jnp.int32, (block, block), 0).astype(jnp.float32)
    across = lax.broadcasted_iota(jnp.int32, (block, block), 1).astype(jnp.float32)
    row_hit = jnp.sum(jnp.where(pos == down, acc[tile(3, 0, block)], 0.0), axis=0, keepdims=True)
    hit[0] = jnp.broadcast_to(row_hit, (8, block))
    col_hit = jnp.sum(
        jnp.where(upright[:, 0:1] == across, acc[tile(0, 0, block)], 0.0), axis=0, keepdims=True
    )
    hit[1] = jnp.broadcast_to(col_hit, (8, block))
    for k in range(3):
        flag_copy(k).wait_recv()

    def live(side, part, k):
        flag = (flag_out if side == 0 else flag_in)[k - 1, 0:1, 0:1]
        return jnp.where(flag > 0, part, NEG)

    def scores(side, slot, k, start, size):
        lines = pl.ds(pl.multiple_of(start, 128), size)
        return live(side, dot_t(own[side], far[slot, lines, :]) * factor, k)

    def score_piece(side, slot, k, index, s):
        part = scores(side, slot, k, s * rows, rows)
        keep(side, index, part, s)
        return part

    def tell_stats(index, part, s):
        largest = jnp.max(part, axis=0, keepdims=True)
        total = jnp.sum(jnp.exp(part - largest), axis=0, keepdims=True)
        line = lax.broadcasted_iota(jnp.int32, (8, rows), 0)
        stat_out[index, :, piece(s)] = jnp.where(line < 4, largest, total)

    def stat_copy(index, slot, offset):
        return pltpu.make_async_remote_copy(
            src_ref=stat_out.at[index],
            dst_ref=stat_in.at[slot],
            send_sem=stat_send_sem.at[index],
            recv_sem=stat_recv_sem.at[slot],
            device_id=at(offset),
            device_id_type=MESH,
        )

    stat_copies = (stat_copy(0, 1, 2), stat_copy(1, 1, 3), stat_copy(2, 0, -3))

    @pl.when(is_first)
    def _():
        def early(s):
            arrived(0, s)
            score_piece(0, 0, 1, 1, s)

        def soon(s):
            arrived(3, s)
            score_piece(1, 3, 1, 4, s)

        loop(PIECES, early)
        loop(PIECES, soon)

    @pl.when(is_second)
    def _():
        def early(s):
            arrived(3, s)
            score_piece(1, 3, 1, 4, s)

        def soon(s):
            arrived(4, s)
            q_on(s).start()
            second_on(s).start()
            score_piece(1, 4, 2, 5, s)

        loop(PIECES, early)
        loop(PIECES, soon)
        loop(PIECES, lambda s: q_pass(s).start())

    def near(s):
        arrived(1, s)

        @pl.when(is_first)
        def _():
            first_on(s).start()

        @pl.when(is_second)
        def _():
            p_on(s).start()

        part = score_piece(0, 1, 2, 2, s)

        @pl.when(is_first)
        def _():
            tell_stats(0, part, s)
            arrived(2, s)
            tell_stats(1, score_piece(0, 2, 3, 6, s), s)

            @pl.when(s == PIECES - 1)
            def _():
                stat_copies[0].start()
                stat_copies[1].start()

            arrived(5, s)
            tell_stats(2, score_piece(1, 5, 3, 5, s), s)

        @pl.when(is_second)
        def _():
            arrived(0, s)
            p_pass(s).start()
            score_piece(0, 0, 1, 1, s)

    loop(PIECES, near)

    @pl.when(is_first)
    def _():
        stat_copies[2].start()

    @pl.when(is_second)
    def _():
        stat_copies[2].wait_recv()

    stat_copies[0].wait_recv()

    def tell(index, src, dst, offset):
        return pltpu.make_async_remote_copy(
            src_ref=src,
            dst_ref=extra if dst is None else heard.at[dst],
            send_sem=said_sem.at[index],
            recv_sem=heard_sem.at[6 if dst is None else dst],
            device_id=at(offset),
            device_id_type=MESH,
        )

    def first_tells(side):
        sign = 1 if side == 0 else -1
        return [
            tell(side * 3 + k - 1, said.at[side], (1 - side) * 3 + k - 1, sign * k)
            for k in (1, 2, 3)
        ]

    def passed_tells():
        up = [tell(6 + k, extra, 3 + k, 2 + k) for k in range(3)]
        return up + [tell(8 + k, heard.at[0], k, -k) for k in (1, 2)]

    def second_tells(side):
        return [tell(side, said.at[side], None if side == 0 else 0, -1)]

    for side in range(2):
        tops = jnp.transpose(top[side])
        largest = jnp.max(tops, axis=0, keepdims=True)
        total = jnp.sum(
            jnp.transpose(mass[side]) * jnp.exp(tops - largest), axis=0, keepdims=True
        )
        other = stat_in[side, 0:1, :]
        both = jnp.maximum(largest, other)
        total = total * jnp.exp(largest - both) + stat_in[side, 4:5, :] * jnp.exp(other - both)
        value = both + jnp.log(total)
        said[side] = jnp.broadcast_to(value, (8, block))

        @pl.when(is_first)
        def _():
            for copy in first_tells(side):
                copy.start()

        @pl.when(is_second)
        def _():
            for copy in second_tells(side):
                copy.start()

        lse[side] = jnp.transpose(jnp.broadcast_to(value, (128, block)))

    row_ref[...] = said[0, 0:1, :] - hit[0, 0:1, :]
    col_ref[...] = said[1, 0:1, :] - hit[1, 0:1, :]

    strips = block // STRIP

    def strip(i):
        return pl.ds(pl.multiple_of(i * STRIP, STRIP), STRIP)

    def weigh(side, index, theirs, i):
        per = stage.shape[2] // block
        at_tile = side * 3 + index if index < 3 else 6
        lanes = pl.ds(at_tile % per * block, block)
        score = acc[0, at_tile // per, strip(i), lanes]
        value = jnp.exp(score - lse[side, strip(i), 0:1]) + jnp.exp(score - theirs)
        if index == 0:
            if side == 0:
                across = lax.broadcasted_iota(jnp.int32, (STRIP, block), 1)
                match = upright[strip(i), 0:1] == across.astype(jnp.float32)
            else:
                lines = lax.broadcasted_iota(jnp.int32, (STRIP, block), 0) + i * STRIP
                match = pos_ref[...] == lines
            value = value - jnp.where(match, 2.0, 0.0)
        weight[at_tile, strip(i), :] = value.astype(jnp.bfloat16)

    def weigh_diagonal(i):
        for side in range(2):
            weigh(side, 0, said[1 - side, 0:1, :], i)

    def told(dst):
        tell(0, said.at[0], dst, 1).wait_recv()

    told(0)

    @pl.when(is_first)
    def _():
        told(None)
        for copy in passed_tells():
            copy.start()

    loop(strips, weigh_diagonal)
    for dst in range(1, 6):
        told(dst)

    def weigh_far(i):
        weigh(0, 1, heard[0, 0:1, :], i)
        weigh(0, 2, heard[1, 0:1, :], i)
        weigh(1, 1, heard[3, 0:1, :], i)
        weigh(1, 2, heard[5 - second, 0:1, :], i)

    loop(strips, weigh_far)

    @pl.when(is_first)
    def _():
        loop(strips, lambda i: weigh(0, 3, heard[2, 0:1, :], i))

    width = stage.shape[2]
    parts = depth // width

    def columns(j):
        return pl.ds(pl.multiple_of(j * width, width), width)

    def early_grads(side):
        def early_grad(j):
            slots = (0, 1) if side == 0 else (3, 5 - second)
            total = jnp.dot(
                weight[side * 3], own[1 - side, :, columns(j)], preferred_element_type=jnp.float32
            )
            for index, slot in enumerate(slots):
                total += jnp.dot(
                    weight[side * 3 + 1 + index],
                    far[slot, :, columns(j)],
                    preferred_element_type=jnp.float32,
                )
            acc[side, j] = total

        loop(parts, early_grad)

    def weigh_late(side, start, size):
        slot = late[side]
        k = 3 if side == 0 else 2 + second
        part = scores(side, slot, k, start, size)
        theirs = heard[slot, 0:1, pl.ds(start, size)]
        value = jnp.exp(part - lse[side, :, 0:1]) + jnp.exp(part - theirs)
        weight[6 + side, :, pl.ds(start, size)] = value.astype(jnp.bfloat16)

    def out_copy(side, j):
        hbm = dq_hbm if side == 0 else dp_hbm
        return pltpu.make_async_copy(
            stage.at[lax.rem(j, 2)], hbm.at[:, columns(j)], stage_sem.at[lax.rem(j, 2)]
        )

    def finish(side):
        def late_grad(j):
            total = acc[side, j] + jnp.dot(
                weight[6 + side], far[late[side], :, columns(j)], preferred_element_type=jnp.float32
            )

            @pl.when(j >= 2)
            def _():
                out_copy(side, j - 2).wait()

            stage[lax.rem(j, 2)] = (total * factor).astype(jnp.bfloat16)
            out_copy(side, j).start()

        loop(parts, late_grad)
        out_copy(side, parts - 2).wait()
        out_copy(side, parts - 1).wait()

    def forward(s):
        @pl.when(is_first)
        def _():
            arrived(4, s)
            q_on(s).start()

    forward(0)
    early_grads(1)
    forward(1)
    early_grads(0)
    forward(2)

    @pl.when(is_first)
    def _():
        finish(0)

    for first, count in ((0, PIECES // 2), (PIECES // 2, 1), (PIECES // 2 + 1, 1)):
        here = range(first, first + count)
        if here[-1] == PIECES - 1:
            forward(PIECES - 1)

        @pl.when(is_second)
        def _():
            for s in here:
                arrived(2, s)
            weigh_late(0, first * rows, count * rows)
            for s in here:
                arrived(5, s)

        weigh_late(1, first * rows, count * rows)

    @pl.when(is_second)
    def _():
        finish(0)

    finish(1)

    for k in range(3):
        flag_copy(k).wait_send()
    for copy in (p_down, q_on):
        loop(PIECES, lambda s: copy(s).wait_send())

    @pl.when(is_first)
    def _():
        for copy in (first_own, first_on):
            loop(PIECES, lambda s: copy(s).wait_send())
        for copy in stat_copies + tuple(first_tells(0) + first_tells(1) + passed_tells()):
            copy.wait_send()

    @pl.when(is_second)
    def _():
        for copy in (q_up, p_on, second_own, second_on, p_pass, q_pass):
            loop(PIECES, lambda s: copy(s).wait_send())
        for copy in second_tells(0) + second_tells(1):
            copy.wait_send()


def local(n, queries, passages, links, positives):
    block, depth = queries.shape
    width = min(2 * block, depth // 2)
    flops = 16 * 2 * block * block * depth
    query_grad, passage_grad, row_loss, col_loss = pl.pallas_call(
        functools.partial(kernel, n),
        out_shape=(
            jax.ShapeDtypeStruct((block, depth), jnp.bfloat16),
            jax.ShapeDtypeStruct((block, depth), jnp.bfloat16),
            jax.ShapeDtypeStruct((1, block), jnp.float32),
            jax.ShapeDtypeStruct((1, block), jnp.float32),
        ),
        in_specs=[
            pl.BlockSpec(memory_space=pl.ANY),
            pl.BlockSpec(memory_space=pl.ANY),
            pl.BlockSpec(memory_space=pltpu.SMEM),
            pl.BlockSpec(memory_space=pltpu.VMEM),
        ],
        out_specs=(
            pl.BlockSpec(memory_space=pl.ANY),
            pl.BlockSpec(memory_space=pl.ANY),
            pl.BlockSpec(memory_space=pltpu.VMEM),
            pl.BlockSpec(memory_space=pltpu.VMEM),
        ),
        scratch_shapes=[
            pltpu.VMEM((2, block, depth), jnp.bfloat16),
            pltpu.VMEM((6, block, depth), jnp.bfloat16),
            pltpu.VMEM((2, max(depth // width, -(-7 * block // width)), block, width), jnp.float32),
            pltpu.VMEM((8, block, block), jnp.bfloat16),
            pltpu.VMEM((2, block, 128), jnp.float32),
            pltpu.VMEM((2, block, 128), jnp.float32),
            pltpu.VMEM((2, block, 128), jnp.float32),
            pltpu.VMEM((2, block, width), jnp.bfloat16),
            pltpu.VMEM((block, 128), jnp.float32),
            pltpu.VMEM((2, 8, block), jnp.float32),
            pltpu.VMEM((2, 8, block), jnp.float32),
            pltpu.VMEM((6, 8, block), jnp.float32),
            pltpu.VMEM((8, block), jnp.float32),
            pltpu.VMEM((3, 8, block), jnp.float32),
            pltpu.VMEM((2, 8, block), jnp.float32),
            pltpu.VMEM((3, 8, 128), jnp.float32),
            pltpu.VMEM((3, 8, 128), jnp.float32),
            pltpu.SemaphoreType.DMA((2,)),
            pltpu.SemaphoreType.DMA((8, PIECES)),
            pltpu.SemaphoreType.DMA((6, PIECES)),
            pltpu.SemaphoreType.DMA((11,)),
            pltpu.SemaphoreType.DMA((7,)),
            pltpu.SemaphoreType.DMA((3,)),
            pltpu.SemaphoreType.DMA((3,)),
            pltpu.SemaphoreType.DMA((3,)),
            pltpu.SemaphoreType.DMA((2,)),
            pltpu.SemaphoreType.DMA((2,)),
        ],
        cost_estimate=pl.CostEstimate(
            flops=flops, bytes_accessed=8 * block * depth, transcendentals=24 * block * block
        ),
        compiler_params=pltpu.CompilerParams(
            collective_id=0, has_side_effects=True, vmem_limit_bytes=60 * 1024 * 1024
        ),
    )(queries, passages, links, positives)
    return query_grad, passage_grad, row_loss.reshape(block), col_loss.reshape(block)


def solution(mesh):
    placed = (P("dp", None), P("dp", None), P("dp", None), P("dp", None))
    return jax.shard_map(
        functools.partial(local, mesh.size),
        mesh=mesh,
        in_specs=placed,
        out_specs=(P("dp", None), P("dp", None), P("dp"), P("dp")),
        check_vma=False,
    )
```

```python
import functools

import jax
import jax.numpy as jnp
from jax import lax
from jax.experimental import pallas as pl
from jax.experimental.pallas import tpu as pltpu
from jax.sharding import PartitionSpec as P

MESH = pl.DeviceIdType.MESH
NEG = -1e30
PIECES = 4
STRIP = 64


def kernel(
    n,
    q_hbm,
    p_hbm,
    links_ref,
    pos_ref,
    dq_hbm,
    dp_hbm,
    row_ref,
    col_ref,
    own,
    far,
    acc,
    weight,
    top,
    mass,
    lse,
    stage,
    upright,
    hit,
    said,
    heard,
    extra,
    stat_out,
    stat_in,
    flag_out,
    flag_in,
    load_sem,
    send_sem,
    recv_sem,
    said_sem,
    heard_sem,
    flag_send_sem,
    flag_recv_sem,
    stat_send_sem,
    stat_recv_sem,
    stage_sem,
):
    block, depth = q_hbm.shape
    factor = depth ** (-0.5)
    rows = block // PIECES
    me = lax.axis_index("dp")
    second = lax.rem(me, 2)
    is_first = second == 0
    is_second = second == 1
    late = (2, 4 + second)

    def at(offset):
        return (lax.rem(me + offset + n, n),)

    barrier = pltpu.get_barrier_semaphore()
    for offset in (1, 2, 3, 4, -1, -2, -3, -4):
        pl.semaphore_signal(barrier, inc=1, device_id=at(offset), device_id_type=MESH)
    pl.semaphore_wait(barrier, 8)

    def piece(s):
        return pl.ds(pl.multiple_of(s * rows, rows), rows)

    def send(stream, s, src, slot, offset):
        return pltpu.make_async_remote_copy(
            src_ref=src.at[piece(s)],
            dst_ref=far.at[slot, piece(s)],
            send_sem=send_sem.at[stream, s],
            recv_sem=recv_sem.at[slot, s],
            device_id=at(offset),
            device_id_type=MESH,
        )

    def q_up(s):
        return send(0, s, q_hbm, 4, 2)

    def p_down(s):
        return send(1, s, p_hbm, 1, -2)

    def p_on(s):
        return send(2, s, far.at[1], 2, -1)

    def q_on(s):
        return send(3, s, far.at[4], 5, 1)

    def first_own(s):
        return send(4, s, q_hbm, 3, 1)

    def first_on(s):
        return send(5, s, far.at[1], 0, 1)

    def second_own(s):
        return send(4, s, p_hbm, 0, -1)

    def second_on(s):
        return send(5, s, far.at[4], 3, -1)

    def q_pass(s):
        return send(7, s, far.at[3], 4, 1)

    def p_pass(s):
        return send(6, s, far.at[0], 2, -2)

    def arrived(slot, s):
        send(0, s, q_hbm, slot, 1).wait_recv()

    def loop(count, body):
        def step(s, carry):
            body(s)
            return carry

        lax.fori_loop(0, count, step, 0)

    for k in range(3):
        flag_out[k] = jnp.full((8, 128), links_ref[0, k].astype(jnp.float32), jnp.float32)

    def flag_copy(k):
        return pltpu.make_async_remote_copy(
            src_ref=flag_out.at[k],
            dst_ref=flag_in.at[k],
            send_sem=flag_send_sem.at[k],
            recv_sem=flag_recv_sem.at[k],
            device_id=at(k + 1),
            device_id_type=MESH,
        )

    for k in range(3):
        flag_copy(k).start()

    @pl.when(is_first)
    def _():
        loop(PIECES, lambda s: p_down(s).start())
        loop(PIECES, lambda s: first_own(s).start())

    @pl.when(is_second)
    def _():
        loop(PIECES, lambda s: q_up(s).start())
        loop(PIECES, lambda s: p_down(s).start())
        loop(PIECES, lambda s: second_own(s).start())

    load_q = pltpu.make_async_copy(q_hbm, own.at[0], load_sem.at[0])
    load_p = pltpu.make_async_copy(p_hbm, own.at[1], load_sem.at[1])
    load_q.start()
    load_p.start()

    pos = pos_ref[...].astype(jnp.float32)
    upright[...] = jnp.transpose(jnp.broadcast_to(pos, (128, block)))
    top[...] = jnp.full(top.shape, NEG, jnp.float32)
    mass[...] = jnp.zeros(mass.shape, jnp.float32)

    @pl.when(is_first)
    def _():
        line = lax.broadcasted_iota(jnp.int32, (8, block), 0)
        stat_in[0] = jnp.where(line < 4, NEG, 0.0)

    load_q.wait()
    load_p.wait()

    def dot_t(a, b):
        return lax.dot_general(a, b, (((1,), (1,)), ((), ())), preferred_element_type=jnp.float32)

    def fold(side, part):
        before = top[side]
        now = jnp.maximum(before, part)
        mass[side] = mass[side] * jnp.exp(before - now) + jnp.exp(part - now)
        top[side] = now

    def tile(index, start, size):
        per = stage.shape[2] // block
        first = lax.rem(index, per) * block + start
        return (0, index // per, slice(None), pl.ds(pl.multiple_of(first, 128), size))

    def keep(side, index, part, s):
        acc[tile(index, s * rows, rows)] = part
        fold(side, part)

    def diagonal(t):
        side, s = t // PIECES, lax.rem(t, PIECES)
        keep(side, side * 3, dot_t(own[side], own[1 - side, piece(s), :]) * factor, s)

    loop(2 * PIECES, diagonal)
    down = lax.broadcasted_iota(jnp.int32, (block, block), 0).astype(jnp.float32)
    across = lax.broadcasted_iota(jnp.int32, (block, block), 1).astype(jnp.float32)
    row_hit = jnp.sum(jnp.where(pos == down, acc[tile(3, 0, block)], 0.0), axis=0, keepdims=True)
    hit[0] = jnp.broadcast_to(row_hit, (8, block))
    col_hit = jnp.sum(
        jnp.where(upright[:, 0:1] == across, acc[tile(0, 0, block)], 0.0), axis=0, keepdims=True
    )
    hit[1] = jnp.broadcast_to(col_hit, (8, block))
    for k in range(3):
        flag_copy(k).wait_recv()

    def live(side, part, k):
        flag = (flag_out if side == 0 else flag_in)[k - 1, 0:1, 0:1]
        return jnp.where(flag > 0, part, NEG)

    def scores(side, slot, k, start, size):
        lines = pl.ds(pl.multiple_of(start, 128), size)
        return live(side, dot_t(own[side], far[slot, lines, :]) * factor, k)

    def score_piece(side, slot, k, index, s):
        part = scores(side, slot, k, s * rows, rows)
        keep(side, index, part, s)
        return part

    def tell_stats(index, part, s):
        largest = jnp.max(part, axis=0, keepdims=True)
        total = jnp.sum(jnp.exp(part - largest), axis=0, keepdims=True)
        line = lax.broadcasted_iota(jnp.int32, (8, rows), 0)
        stat_out[index, :, piece(s)] = jnp.where(line < 4, largest, total)

    def stat_copy(index, slot, offset):
        return pltpu.make_async_remote_copy(
            src_ref=stat_out.at[index],
            dst_ref=stat_in.at[slot],
            send_sem=stat_send_sem.at[index],
            recv_sem=stat_recv_sem.at[slot],
            device_id=at(offset),
            device_id_type=MESH,
        )

    stat_copies = (stat_copy(0, 1, 2), stat_copy(1, 1, 3), stat_copy(2, 0, -3))

    @pl.when(is_first)
    def _():
        def early(s):
            arrived(0, s)
            score_piece(0, 0, 1, 1, s)

        def soon(s):
            arrived(3, s)
            score_piece(1, 3, 1, 4, s)

        loop(PIECES, early)
        loop(PIECES, soon)

    @pl.when(is_second)
    def _():
        def early(s):
            arrived(3, s)
            score_piece(1, 3, 1, 4, s)

        def soon(s):
            arrived(4, s)
            q_on(s).start()
            second_on(s).start()
            score_piece(1, 4, 2, 5, s)

        loop(PIECES, early)
        loop(PIECES, soon)
        loop(PIECES, lambda s: q_pass(s).start())

    def near(s):
        arrived(1, s)

        @pl.when(is_first)
        def _():
            first_on(s).start()

        @pl.when(is_second)
        def _():
            p_on(s).start()

        part = score_piece(0, 1, 2, 2, s)

        @pl.when(is_first)
        def _():
            tell_stats(0, part, s)
            arrived(2, s)
            tell_stats(1, score_piece(0, 2, 3, 6, s), s)

            @pl.when(s == PIECES - 1)
            def _():
                stat_copies[0].start()
                stat_copies[1].start()

            arrived(5, s)
            tell_stats(2, score_piece(1, 5, 3, 5, s), s)

        @pl.when(is_second)
        def _():
            arrived(0, s)
            p_pass(s).start()
            score_piece(0, 0, 1, 1, s)

    loop(PIECES, near)

    @pl.when(is_first)
    def _():
        stat_copies[2].start()

    @pl.when(is_second)
    def _():
        stat_copies[2].wait_recv()

    stat_copies[0].wait_recv()

    def tell(index, src, dst, offset):
        return pltpu.make_async_remote_copy(
            src_ref=src,
            dst_ref=extra if dst is None else heard.at[dst],
            send_sem=said_sem.at[index],
            recv_sem=heard_sem.at[6 if dst is None else dst],
            device_id=at(offset),
            device_id_type=MESH,
        )

    def first_tells(side):
        sign = 1 if side == 0 else -1
        return [
            tell(side * 3 + k - 1, said.at[side], (1 - side) * 3 + k - 1, sign * k)
            for k in (1, 2, 3)
        ]

    def passed_tells():
        up = [tell(6 + k, extra, 3 + k, 2 + k) for k in range(3)]
        return up + [tell(8 + k, heard.at[0], k, -k) for k in (1, 2)]

    def second_tells(side):
        return [tell(side, said.at[side], None if side == 0 else 0, -1)]

    for side in range(2):
        tops = jnp.transpose(top[side])
        largest = jnp.max(tops, axis=0, keepdims=True)
        total = jnp.sum(
            jnp.transpose(mass[side]) * jnp.exp(tops - largest), axis=0, keepdims=True
        )
        other = stat_in[side, 0:1, :]
        both = jnp.maximum(largest, other)
        total = total * jnp.exp(largest - both) + stat_in[side, 4:5, :] * jnp.exp(other - both)
        value = both + jnp.log(total)
        said[side] = jnp.broadcast_to(value, (8, block))

        @pl.when(is_first)
        def _():
            for copy in first_tells(side):
                copy.start()

        @pl.when(is_second)
        def _():
            for copy in second_tells(side):
                copy.start()

        lse[side] = jnp.transpose(jnp.broadcast_to(value, (128, block)))

    row_ref[...] = said[0, 0:1, :] - hit[0, 0:1, :]
    col_ref[...] = said[1, 0:1, :] - hit[1, 0:1, :]

    strips = block // STRIP

    def strip(i):
        return pl.ds(pl.multiple_of(i * STRIP, STRIP), STRIP)

    def weigh(side, index, theirs, i):
        per = stage.shape[2] // block
        at_tile = side * 3 + index if index < 3 else 6
        lanes = pl.ds(at_tile % per * block, block)
        score = acc[0, at_tile // per, strip(i), lanes]
        value = jnp.exp(score - lse[side, strip(i), 0:1]) + jnp.exp(score - theirs)
        if index == 0:
            if side == 0:
                across = lax.broadcasted_iota(jnp.int32, (STRIP, block), 1)
                match = upright[strip(i), 0:1] == across.astype(jnp.float32)
            else:
                lines = lax.broadcasted_iota(jnp.int32, (STRIP, block), 0) + i * STRIP
                match = pos_ref[...] == lines
            value = value - jnp.where(match, 2.0, 0.0)
        weight[at_tile, strip(i), :] = value.astype(jnp.bfloat16)

    def weigh_diagonal(i):
        for side in range(2):
            weigh(side, 0, said[1 - side, 0:1, :], i)

    def told(dst):
        tell(0, said.at[0], dst, 1).wait_recv()

    told(0)

    @pl.when(is_first)
    def _():
        told(None)
        for copy in passed_tells():
            copy.start()

    loop(strips, weigh_diagonal)
    for dst in range(1, 6):
        told(dst)

    def weigh_far(i):
        weigh(0, 1, heard[0, 0:1, :], i)
        weigh(0, 2, heard[1, 0:1, :], i)
        weigh(1, 1, heard[3, 0:1, :], i)
        weigh(1, 2, heard[5 - second, 0:1, :], i)

    loop(strips, weigh_far)

    @pl.when(is_first)
    def _():
        loop(strips, lambda i: weigh(0, 3, heard[2, 0:1, :], i))

    width = stage.shape[2]
    parts = depth // width

    def columns(j):
        return pl.ds(pl.multiple_of(j * width, width), width)

    def early_grads(side):
        def early_grad(j):
            slots = (0, 1) if side == 0 else (3, 5 - second)
            total = jnp.dot(
                weight[side * 3], own[1 - side, :, columns(j)], preferred_element_type=jnp.float32
            )
            for index, slot in enumerate(slots):
                total += jnp.dot(
                    weight[side * 3 + 1 + index],
                    far[slot, :, columns(j)],
                    preferred_element_type=jnp.float32,
                )
            acc[side, j] = total

        loop(parts, early_grad)

    def weigh_late(side, start, size):
        slot = late[side]
        k = 3 if side == 0 else 2 + second
        part = scores(side, slot, k, start, size)
        theirs = heard[slot, 0:1, pl.ds(start, size)]
        value = jnp.exp(part - lse[side, :, 0:1]) + jnp.exp(part - theirs)
        weight[6 + side, :, pl.ds(start, size)] = value.astype(jnp.bfloat16)

    def out_copy(side, j):
        hbm = dq_hbm if side == 0 else dp_hbm
        return pltpu.make_async_copy(
            stage.at[lax.rem(j, 2)], hbm.at[:, columns(j)], stage_sem.at[lax.rem(j, 2)]
        )

    half = block // 2

    def late_dot(side, start, j):
        return jnp.dot(
            weight[6 + side, :, start : start + half],
            far[late[side], start : start + half, columns(j)],
            preferred_element_type=jnp.float32,
        )

    def begin(side):
        def first_half(j):
            acc[side, j] += late_dot(side, 0, j)

        loop(parts, first_half)

    def finish(side):
        def late_grad(j):
            total = acc[side, j] + late_dot(side, half, j)

            @pl.when(j >= 2)
            def _():
                out_copy(side, j - 2).wait()

            if side == 1:

                @pl.when(j < 2)
                def _():
                    out_copy(0, parts - 2 + j).wait()

            stage[lax.rem(j, 2)] = (total * factor).astype(jnp.bfloat16)
            out_copy(side, j).start()

        loop(parts, late_grad)

    def forward(s):
        @pl.when(is_first)
        def _():
            arrived(4, s)
            q_on(s).start()

    forward(0)
    early_grads(1)
    forward(1)
    early_grads(0)
    forward(2)

    @pl.when(is_first)
    def _():
        begin(0)
        finish(0)

    def late_pieces(side, first, count):
        if side == 1:
            for s in range(first, first + count):
                if s == PIECES - 1:
                    forward(s)

        @pl.when(is_second)
        def _():
            for s in range(first, first + count):
                arrived(2 if side == 0 else 5, s)
            if side == 0:
                weigh_late(0, first * rows, count * rows)

        if side == 1:
            weigh_late(1, first * rows, count * rows)

    late_pieces(0, 0, PIECES // 2)
    late_pieces(1, 0, PIECES // 2)

    @pl.when(is_second)
    def _():
        begin(0)

    begin(1)
    late_pieces(0, PIECES // 2, 1)
    late_pieces(1, PIECES // 2, 1)
    late_pieces(0, PIECES // 2 + 1, 1)

    @pl.when(is_second)
    def _():
        finish(0)

    late_pieces(1, PIECES // 2 + 1, 1)
    finish(1)
    out_copy(1, parts - 2).wait()
    out_copy(1, parts - 1).wait()

    for k in range(3):
        flag_copy(k).wait_send()
    for copy in (p_down, q_on):
        loop(PIECES, lambda s: copy(s).wait_send())

    @pl.when(is_first)
    def _():
        for copy in (first_own, first_on):
            loop(PIECES, lambda s: copy(s).wait_send())
        for copy in stat_copies + tuple(first_tells(0) + first_tells(1) + passed_tells()):
            copy.wait_send()

    @pl.when(is_second)
    def _():
        for copy in (q_up, p_on, second_own, second_on, p_pass, q_pass):
            loop(PIECES, lambda s: copy(s).wait_send())
        for copy in second_tells(0) + second_tells(1):
            copy.wait_send()


def local(n, queries, passages, links, positives):
    block, depth = queries.shape
    width = min(2 * block, depth // 2)
    flops = 16 * 2 * block * block * depth
    query_grad, passage_grad, row_loss, col_loss = pl.pallas_call(
        functools.partial(kernel, n),
        out_shape=(
            jax.ShapeDtypeStruct((block, depth), jnp.bfloat16),
            jax.ShapeDtypeStruct((block, depth), jnp.bfloat16),
            jax.ShapeDtypeStruct((1, block), jnp.float32),
            jax.ShapeDtypeStruct((1, block), jnp.float32),
        ),
        in_specs=[
            pl.BlockSpec(memory_space=pl.ANY),
            pl.BlockSpec(memory_space=pl.ANY),
            pl.BlockSpec(memory_space=pltpu.SMEM),
            pl.BlockSpec(memory_space=pltpu.VMEM),
        ],
        out_specs=(
            pl.BlockSpec(memory_space=pl.ANY),
            pl.BlockSpec(memory_space=pl.ANY),
            pl.BlockSpec(memory_space=pltpu.VMEM),
            pl.BlockSpec(memory_space=pltpu.VMEM),
        ),
        scratch_shapes=[
            pltpu.VMEM((2, block, depth), jnp.bfloat16),
            pltpu.VMEM((6, block, depth), jnp.bfloat16),
            pltpu.VMEM((2, max(depth // width, -(-7 * block // width)), block, width), jnp.float32),
            pltpu.VMEM((8, block, block), jnp.bfloat16),
            pltpu.VMEM((2, block, 128), jnp.float32),
            pltpu.VMEM((2, block, 128), jnp.float32),
            pltpu.VMEM((2, block, 128), jnp.float32),
            pltpu.VMEM((2, block, width), jnp.bfloat16),
            pltpu.VMEM((block, 128), jnp.float32),
            pltpu.VMEM((2, 8, block), jnp.float32),
            pltpu.VMEM((2, 8, block), jnp.float32),
            pltpu.VMEM((6, 8, block), jnp.float32),
            pltpu.VMEM((8, block), jnp.float32),
            pltpu.VMEM((3, 8, block), jnp.float32),
            pltpu.VMEM((2, 8, block), jnp.float32),
            pltpu.VMEM((3, 8, 128), jnp.float32),
            pltpu.VMEM((3, 8, 128), jnp.float32),
            pltpu.SemaphoreType.DMA((2,)),
            pltpu.SemaphoreType.DMA((8, PIECES)),
            pltpu.SemaphoreType.DMA((6, PIECES)),
            pltpu.SemaphoreType.DMA((11,)),
            pltpu.SemaphoreType.DMA((7,)),
            pltpu.SemaphoreType.DMA((3,)),
            pltpu.SemaphoreType.DMA((3,)),
            pltpu.SemaphoreType.DMA((3,)),
            pltpu.SemaphoreType.DMA((2,)),
            pltpu.SemaphoreType.DMA((2,)),
        ],
        cost_estimate=pl.CostEstimate(
            flops=flops, bytes_accessed=8 * block * depth, transcendentals=24 * block * block
        ),
        compiler_params=pltpu.CompilerParams(
            collective_id=0, has_side_effects=True, vmem_limit_bytes=60 * 1024 * 1024
        ),
    )(queries, passages, links, positives)
    return query_grad, passage_grad, row_loss.reshape(block), col_loss.reshape(block)


def solution(mesh):
    placed = (P("dp", None), P("dp", None), P("dp", None), P("dp", None))
    return jax.shard_map(
        functools.partial(local, mesh.size),
        mesh=mesh,
        in_specs=placed,
        out_specs=(P("dp", None), P("dp", None), P("dp"), P("dp")),
        check_vma=False,
    )
```

```python
import functools

import jax
import jax.numpy as jnp
from jax import lax
from jax.experimental import pallas as pl
from jax.experimental.pallas import tpu as pltpu
from jax.sharding import PartitionSpec as P

MESH = pl.DeviceIdType.MESH
NEG = -1e30
PIECES = 4
STRIP = 64


def kernel(
    n,
    q_hbm,
    p_hbm,
    links_ref,
    pos_ref,
    dq_ref,
    dp_ref,
    row_ref,
    col_ref,
    own,
    far,
    acc,
    weight,
    top,
    mass,
    lse,
    upright,
    hit,
    said,
    heard,
    extra,
    stat_out,
    stat_in,
    flag_out,
    flag_in,
    load_sem,
    send_sem,
    recv_sem,
    said_sem,
    heard_sem,
    flag_send_sem,
    flag_recv_sem,
    stat_send_sem,
    stat_recv_sem,
):
    block, depth = q_hbm.shape
    factor = depth ** (-0.5)
    rows = block // PIECES
    me = lax.axis_index("dp")
    second = lax.rem(me, 2)
    is_first = second == 0
    is_second = second == 1
    late = (2, 4 + second)

    def at(offset):
        return (lax.rem(me + offset + n, n),)

    barrier = pltpu.get_barrier_semaphore()
    for offset in (1, 2, 3, 4, -1, -2, -3, -4):
        pl.semaphore_signal(barrier, inc=1, device_id=at(offset), device_id_type=MESH)
    pl.semaphore_wait(barrier, 8)

    def piece(s):
        return pl.ds(pl.multiple_of(s * rows, rows), rows)

    def send(stream, s, src, slot, offset):
        return pltpu.make_async_remote_copy(
            src_ref=src.at[piece(s)],
            dst_ref=far.at[slot, piece(s)],
            send_sem=send_sem.at[stream, s],
            recv_sem=recv_sem.at[slot, s],
            device_id=at(offset),
            device_id_type=MESH,
        )

    def q_up(s):
        return send(0, s, q_hbm, 4, 2)

    def p_down(s):
        return send(1, s, p_hbm, 1, -2)

    def p_on(s):
        return send(2, s, far.at[1], 2, -1)

    def q_on(s):
        return send(3, s, far.at[4], 5, 1)

    def first_own(s):
        return send(4, s, q_hbm, 3, 1)

    def first_on(s):
        return send(5, s, far.at[1], 0, 1)

    def second_own(s):
        return send(4, s, p_hbm, 0, -1)

    def second_on(s):
        return send(5, s, far.at[4], 3, -1)

    def q_pass(s):
        return send(7, s, far.at[3], 4, 1)

    def p_pass(s):
        return send(6, s, far.at[0], 2, -2)

    def arrived(slot, s):
        send(0, s, q_hbm, slot, 1).wait_recv()

    def loop(count, body):
        def step(s, carry):
            body(s)
            return carry

        lax.fori_loop(0, count, step, 0)

    for k in range(3):
        flag_out[k] = jnp.full((8, 128), links_ref[0, k].astype(jnp.float32), jnp.float32)

    def flag_copy(k):
        return pltpu.make_async_remote_copy(
            src_ref=flag_out.at[k],
            dst_ref=flag_in.at[k],
            send_sem=flag_send_sem.at[k],
            recv_sem=flag_recv_sem.at[k],
            device_id=at(k + 1),
            device_id_type=MESH,
        )

    for k in range(3):
        flag_copy(k).start()

    @pl.when(is_first)
    def _():
        loop(PIECES, lambda s: p_down(s).start())
        loop(PIECES, lambda s: first_own(s).start())

    @pl.when(is_second)
    def _():
        loop(PIECES, lambda s: q_up(s).start())
        loop(PIECES, lambda s: p_down(s).start())
        loop(PIECES, lambda s: second_own(s).start())

    load_q = pltpu.make_async_copy(q_hbm, own.at[0], load_sem.at[0])
    load_p = pltpu.make_async_copy(p_hbm, own.at[1], load_sem.at[1])
    load_q.start()
    load_p.start()

    pos = pos_ref[...].astype(jnp.float32)
    upright[...] = jnp.transpose(jnp.broadcast_to(pos, (128, block)))
    top[...] = jnp.full(top.shape, NEG, jnp.float32)
    mass[...] = jnp.zeros(mass.shape, jnp.float32)

    @pl.when(is_first)
    def _():
        line = lax.broadcasted_iota(jnp.int32, (8, block), 0)
        stat_in[0] = jnp.where(line < 4, NEG, 0.0)

    load_q.wait()
    load_p.wait()

    def dot_t(a, b):
        return lax.dot_general(a, b, (((1,), (1,)), ((), ())), preferred_element_type=jnp.float32)

    def fold(side, part):
        before = top[side]
        now = jnp.maximum(before, part)
        mass[side] = mass[side] * jnp.exp(before - now) + jnp.exp(part - now)
        top[side] = now

    def tile(index, start, size):
        per = acc.shape[3] // block
        first = lax.rem(index, per) * block + start
        return (0, index // per, slice(None), pl.ds(pl.multiple_of(first, 128), size))

    def keep(side, index, part, s):
        acc[tile(index, s * rows, rows)] = part
        fold(side, part)

    def diagonal(t):
        side, s = t // PIECES, lax.rem(t, PIECES)
        keep(side, side * 3, dot_t(own[side], own[1 - side, piece(s), :]) * factor, s)

    loop(2 * PIECES, diagonal)
    down = lax.broadcasted_iota(jnp.int32, (block, block), 0).astype(jnp.float32)
    across = lax.broadcasted_iota(jnp.int32, (block, block), 1).astype(jnp.float32)
    row_hit = jnp.sum(jnp.where(pos == down, acc[tile(3, 0, block)], 0.0), axis=0, keepdims=True)
    hit[0] = jnp.broadcast_to(row_hit, (8, block))
    col_hit = jnp.sum(
        jnp.where(upright[:, 0:1] == across, acc[tile(0, 0, block)], 0.0), axis=0, keepdims=True
    )
    hit[1] = jnp.broadcast_to(col_hit, (8, block))
    for k in range(3):
        flag_copy(k).wait_recv()

    def live(side, part, k):
        flag = (flag_out if side == 0 else flag_in)[k - 1, 0:1, 0:1]
        return jnp.where(flag > 0, part, NEG)

    def scores(side, slot, k, start, size):
        lines = pl.ds(pl.multiple_of(start, 128), size)
        return live(side, dot_t(own[side], far[slot, lines, :]) * factor, k)

    def score_piece(side, slot, k, index, s):
        part = scores(side, slot, k, s * rows, rows)
        keep(side, index, part, s)
        return part

    def tell_stats(index, part, s):
        largest = jnp.max(part, axis=0, keepdims=True)
        total = jnp.sum(jnp.exp(part - largest), axis=0, keepdims=True)
        line = lax.broadcasted_iota(jnp.int32, (8, rows), 0)
        stat_out[index, :, piece(s)] = jnp.where(line < 4, largest, total)

    def stat_copy(index, slot, offset):
        return pltpu.make_async_remote_copy(
            src_ref=stat_out.at[index],
            dst_ref=stat_in.at[slot],
            send_sem=stat_send_sem.at[index],
            recv_sem=stat_recv_sem.at[slot],
            device_id=at(offset),
            device_id_type=MESH,
        )

    stat_copies = (stat_copy(0, 1, 2), stat_copy(1, 1, 3), stat_copy(2, 0, -3))

    @pl.when(is_first)
    def _():
        def early(s):
            arrived(0, s)
            score_piece(0, 0, 1, 1, s)

        def soon(s):
            arrived(3, s)
            score_piece(1, 3, 1, 4, s)

        loop(PIECES, early)
        loop(PIECES, soon)

    @pl.when(is_second)
    def _():
        def early(s):
            arrived(3, s)
            score_piece(1, 3, 1, 4, s)

        def soon(s):
            arrived(4, s)
            q_on(s).start()
            second_on(s).start()
            score_piece(1, 4, 2, 5, s)

        loop(PIECES, early)
        loop(PIECES, soon)
        loop(PIECES, lambda s: q_pass(s).start())

    def near(s):
        arrived(1, s)

        @pl.when(is_first)
        def _():
            first_on(s).start()

        @pl.when(is_second)
        def _():
            p_on(s).start()

        part = score_piece(0, 1, 2, 2, s)

        @pl.when(is_first)
        def _():
            tell_stats(0, part, s)
            arrived(2, s)
            tell_stats(1, score_piece(0, 2, 3, 6, s), s)

            @pl.when(s == PIECES - 1)
            def _():
                stat_copies[0].start()
                stat_copies[1].start()

            arrived(5, s)
            tell_stats(2, score_piece(1, 5, 3, 5, s), s)

        @pl.when(is_second)
        def _():
            arrived(0, s)
            p_pass(s).start()
            score_piece(0, 0, 1, 1, s)

    loop(PIECES, near)

    @pl.when(is_first)
    def _():
        stat_copies[2].start()

    @pl.when(is_second)
    def _():
        stat_copies[2].wait_recv()

    stat_copies[0].wait_recv()

    def tell(index, src, dst, offset):
        return pltpu.make_async_remote_copy(
            src_ref=src,
            dst_ref=extra if dst is None else heard.at[dst],
            send_sem=said_sem.at[index],
            recv_sem=heard_sem.at[6 if dst is None else dst],
            device_id=at(offset),
            device_id_type=MESH,
        )

    def first_tells(side):
        sign = 1 if side == 0 else -1
        return [
            tell(side * 3 + k - 1, said.at[side], (1 - side) * 3 + k - 1, sign * k)
            for k in (1, 2, 3)
        ]

    def passed_tells():
        up = [tell(6 + k, extra, 3 + k, 2 + k) for k in range(3)]
        return up + [tell(8 + k, heard.at[0], k, -k) for k in (1, 2)]

    def second_tells(side):
        return [tell(side, said.at[side], None if side == 0 else 0, -1)]

    for side in range(2):
        tops = jnp.transpose(top[side])
        largest = jnp.max(tops, axis=0, keepdims=True)
        total = jnp.sum(
            jnp.transpose(mass[side]) * jnp.exp(tops - largest), axis=0, keepdims=True
        )
        other = stat_in[side, 0:1, :]
        both = jnp.maximum(largest, other)
        total = total * jnp.exp(largest - both) + stat_in[side, 4:5, :] * jnp.exp(other - both)
        value = both + jnp.log(total)
        said[side] = jnp.broadcast_to(value, (8, block))

        @pl.when(is_first)
        def _():
            for copy in first_tells(side):
                copy.start()

        @pl.when(is_second)
        def _():
            for copy in second_tells(side):
                copy.start()

        lse[side] = jnp.transpose(jnp.broadcast_to(value, (128, block)))

    row_ref[...] = said[0, 0:1, :] - hit[0, 0:1, :]
    col_ref[...] = said[1, 0:1, :] - hit[1, 0:1, :]

    strips = block // STRIP

    def strip(i):
        return pl.ds(pl.multiple_of(i * STRIP, STRIP), STRIP)

    def weigh(side, index, theirs, i):
        per = acc.shape[3] // block
        at_tile = side * 3 + index if index < 3 else 6
        lanes = pl.ds(at_tile % per * block, block)
        score = acc[0, at_tile // per, strip(i), lanes]
        value = jnp.exp(score - lse[side, strip(i), 0:1]) + jnp.exp(score - theirs)
        if index == 0:
            if side == 0:
                across = lax.broadcasted_iota(jnp.int32, (STRIP, block), 1)
                match = upright[strip(i), 0:1] == across.astype(jnp.float32)
            else:
                lines = lax.broadcasted_iota(jnp.int32, (STRIP, block), 0) + i * STRIP
                match = pos_ref[...] == lines
            value = value - jnp.where(match, 2.0, 0.0)
        weight[at_tile, strip(i), :] = value.astype(jnp.bfloat16)

    def weigh_diagonal(i):
        for side in range(2):
            weigh(side, 0, said[1 - side, 0:1, :], i)

    def told(dst):
        tell(0, said.at[0], dst, 1).wait_recv()

    told(0)

    @pl.when(is_first)
    def _():
        told(None)
        for copy in passed_tells():
            copy.start()

    loop(strips, weigh_diagonal)
    for dst in range(1, 6):
        told(dst)

    def weigh_far(i):
        weigh(0, 1, heard[0, 0:1, :], i)
        weigh(0, 2, heard[1, 0:1, :], i)
        weigh(1, 1, heard[3, 0:1, :], i)
        weigh(1, 2, heard[5 - second, 0:1, :], i)

    loop(strips, weigh_far)

    @pl.when(is_first)
    def _():
        loop(strips, lambda i: weigh(0, 3, heard[2, 0:1, :], i))

    width = acc.shape[3]
    parts = depth // width

    def columns(j):
        return pl.ds(pl.multiple_of(j * width, width), width)

    def early_grads(side):
        def early_grad(j):
            slots = (0, 1) if side == 0 else (3, 5 - second)
            total = jnp.dot(
                weight[side * 3], own[1 - side, :, columns(j)], preferred_element_type=jnp.float32
            )
            for index, slot in enumerate(slots):
                total += jnp.dot(
                    weight[side * 3 + 1 + index],
                    far[slot, :, columns(j)],
                    preferred_element_type=jnp.float32,
                )
            acc[side, j] = total

        loop(parts, early_grad)

    def weigh_late(side, start, size):
        slot = late[side]
        k = 3 if side == 0 else 2 + second
        part = scores(side, slot, k, start, size)
        theirs = heard[slot, 0:1, pl.ds(start, size)]
        value = jnp.exp(part - lse[side, :, 0:1]) + jnp.exp(part - theirs)
        weight[6 + side, :, pl.ds(start, size)] = value.astype(jnp.bfloat16)

    half = block // 2

    def late_dot(side, start, j):
        return jnp.dot(
            weight[6 + side, :, start : start + half],
            far[late[side], start : start + half, columns(j)],
            preferred_element_type=jnp.float32,
        )

    def begin(side):
        def first_half(j):
            acc[side, j] += late_dot(side, 0, j)

        loop(parts, first_half)

    def finish(side):
        def late_grad(j):
            total = acc[side, j] + late_dot(side, half, j)

            out = dq_ref if side == 0 else dp_ref
            out[:, columns(j)] = (total * factor).astype(jnp.bfloat16)

        loop(parts, late_grad)

    def forward(s):
        @pl.when(is_first)
        def _():
            arrived(4, s)
            q_on(s).start()

    forward(0)
    early_grads(1)
    forward(1)
    early_grads(0)
    forward(2)

    @pl.when(is_first)
    def _():
        begin(0)
        finish(0)

    def late_pieces(side, first, count):
        if side == 1:
            for s in range(first, first + count):
                if s == PIECES - 1:
                    forward(s)

        @pl.when(is_second)
        def _():
            for s in range(first, first + count):
                arrived(2 if side == 0 else 5, s)
            if side == 0:
                weigh_late(0, first * rows, count * rows)

        if side == 1:
            weigh_late(1, first * rows, count * rows)

    late_pieces(0, 0, PIECES // 2)
    late_pieces(1, 0, PIECES // 2)

    @pl.when(is_second)
    def _():
        begin(0)

    begin(1)
    late_pieces(0, PIECES // 2, 1)
    late_pieces(1, PIECES // 2, 1)
    late_pieces(0, PIECES // 2 + 1, 1)

    @pl.when(is_second)
    def _():
        finish(0)

    late_pieces(1, PIECES // 2 + 1, 1)
    finish(1)

    for k in range(3):
        flag_copy(k).wait_send()
    for copy in (p_down, q_on):
        loop(PIECES, lambda s: copy(s).wait_send())

    @pl.when(is_first)
    def _():
        for copy in (first_own, first_on):
            loop(PIECES, lambda s: copy(s).wait_send())
        for copy in stat_copies + tuple(first_tells(0) + first_tells(1) + passed_tells()):
            copy.wait_send()

    @pl.when(is_second)
    def _():
        for copy in (q_up, p_on, second_own, second_on, p_pass, q_pass):
            loop(PIECES, lambda s: copy(s).wait_send())
        for copy in second_tells(0) + second_tells(1):
            copy.wait_send()


def local(n, queries, passages, links, positives):
    block, depth = queries.shape
    width = min(2 * block, depth // 2)
    flops = 16 * 2 * block * block * depth
    query_grad, passage_grad, row_loss, col_loss = pl.pallas_call(
        functools.partial(kernel, n),
        out_shape=(
            pltpu.VMEM((block, depth), jnp.bfloat16),
            pltpu.VMEM((block, depth), jnp.bfloat16),
            pltpu.VMEM((1, block), jnp.float32),
            pltpu.VMEM((1, block), jnp.float32),
        ),
        in_specs=[
            pl.BlockSpec(memory_space=pl.ANY),
            pl.BlockSpec(memory_space=pl.ANY),
            pl.BlockSpec(memory_space=pltpu.SMEM),
            pl.BlockSpec(memory_space=pltpu.VMEM),
        ],
        out_specs=(
            pl.BlockSpec(memory_space=pltpu.VMEM),
            pl.BlockSpec(memory_space=pltpu.VMEM),
            pl.BlockSpec(memory_space=pltpu.VMEM),
            pl.BlockSpec(memory_space=pltpu.VMEM),
        ),
        scratch_shapes=[
            pltpu.VMEM((2, block, depth), jnp.bfloat16),
            pltpu.VMEM((6, block, depth), jnp.bfloat16),
            pltpu.VMEM((2, max(depth // width, -(-7 * block // width)), block, width), jnp.float32),
            pltpu.VMEM((8, block, block), jnp.bfloat16),
            pltpu.VMEM((2, block, 128), jnp.float32),
            pltpu.VMEM((2, block, 128), jnp.float32),
            pltpu.VMEM((2, block, 128), jnp.float32),
            pltpu.VMEM((block, 128), jnp.float32),
            pltpu.VMEM((2, 8, block), jnp.float32),
            pltpu.VMEM((2, 8, block), jnp.float32),
            pltpu.VMEM((6, 8, block), jnp.float32),
            pltpu.VMEM((8, block), jnp.float32),
            pltpu.VMEM((3, 8, block), jnp.float32),
            pltpu.VMEM((2, 8, block), jnp.float32),
            pltpu.VMEM((3, 8, 128), jnp.float32),
            pltpu.VMEM((3, 8, 128), jnp.float32),
            pltpu.SemaphoreType.DMA((2,)),
            pltpu.SemaphoreType.DMA((8, PIECES)),
            pltpu.SemaphoreType.DMA((6, PIECES)),
            pltpu.SemaphoreType.DMA((11,)),
            pltpu.SemaphoreType.DMA((7,)),
            pltpu.SemaphoreType.DMA((3,)),
            pltpu.SemaphoreType.DMA((3,)),
            pltpu.SemaphoreType.DMA((3,)),
            pltpu.SemaphoreType.DMA((2,)),
        ],
        cost_estimate=pl.CostEstimate(
            flops=flops, bytes_accessed=8 * block * depth, transcendentals=24 * block * block
        ),
        compiler_params=pltpu.CompilerParams(
            collective_id=0, has_side_effects=True, vmem_limit_bytes=55 * 1024 * 1024
        ),
    )(queries, passages, links, positives)
    return query_grad, passage_grad, row_loss.reshape(block), col_loss.reshape(block)


def solution(mesh):
    placed = (P("dp", None), P("dp", None), P("dp", None), P("dp", None))
    return jax.shard_map(
        functools.partial(local, mesh.size),
        mesh=mesh,
        in_specs=placed,
        out_specs=(P("dp", None), P("dp", None), P("dp"), P("dp")),
        check_vma=False,
    )
```

```python
import functools

import jax
import jax.numpy as jnp
from jax import lax
from jax.experimental import pallas as pl
from jax.experimental.pallas import tpu as pltpu
from jax.sharding import PartitionSpec as P

MESH = pl.DeviceIdType.MESH
NEG = -1e30
PIECES = 4
STRIP = 64


def kernel(
    n,
    q_hbm,
    p_hbm,
    links_ref,
    pos_ref,
    dq_ref,
    dp_ref,
    row_ref,
    col_ref,
    own,
    far,
    acc,
    weight,
    top,
    mass,
    lse,
    upright,
    hit,
    said,
    heard,
    extra,
    stat_out,
    stat_in,
    flag_out,
    flag_in,
    load_sem,
    send_sem,
    recv_sem,
    said_sem,
    heard_sem,
    flag_send_sem,
    flag_recv_sem,
    stat_send_sem,
    stat_recv_sem,
):
    block, depth = q_hbm.shape
    factor = depth ** (-0.5)
    rows = block // PIECES
    me = lax.axis_index("dp")
    second = lax.rem(me, 2)
    is_first = second == 0
    is_second = second == 1
    late = (2, 4 + second)

    def at(offset):
        return (lax.rem(me + offset + n, n),)

    barrier = pltpu.get_barrier_semaphore()
    for offset in (1, 2, 3, 4, -1, -2, -3, -4):
        pl.semaphore_signal(barrier, inc=1, device_id=at(offset), device_id_type=MESH)
    pl.semaphore_wait(barrier, 8)

    def piece(s):
        return pl.ds(pl.multiple_of(s * rows, rows), rows)

    def send(stream, s, src, slot, offset):
        return pltpu.make_async_remote_copy(
            src_ref=src.at[piece(s)],
            dst_ref=far.at[slot, piece(s)],
            send_sem=send_sem.at[stream, s],
            recv_sem=recv_sem.at[slot, s],
            device_id=at(offset),
            device_id_type=MESH,
        )

    def q_up(s):
        return send(0, s, q_hbm, 4, 2)

    def p_down(s):
        return send(1, s, p_hbm, 1, -2)

    def p_on(s):
        return send(2, s, far.at[1], 2, -1)

    def q_on(s):
        return send(3, s, far.at[4], 5, 1)

    def first_own(s):
        return send(4, s, q_hbm, 3, 1)

    def first_on(s):
        return send(5, s, far.at[1], 0, 1)

    def second_own(s):
        return send(4, s, p_hbm, 0, -1)

    def second_on(s):
        return send(5, s, far.at[4], 3, -1)

    def q_pass(s):
        return send(7, s, far.at[3], 4, 1)

    def p_pass(s):
        return send(6, s, far.at[0], 2, -2)

    def arrived(slot, s):
        send(0, s, q_hbm, slot, 1).wait_recv()

    def loop(count, body):
        def step(s, carry):
            body(s)
            return carry

        lax.fori_loop(0, count, step, 0)

    for k in range(3):
        flag_out[k] = jnp.full((8, 128), links_ref[0, k].astype(jnp.float32), jnp.float32)

    def flag_copy(k):
        return pltpu.make_async_remote_copy(
            src_ref=flag_out.at[k],
            dst_ref=flag_in.at[k],
            send_sem=flag_send_sem.at[k],
            recv_sem=flag_recv_sem.at[k],
            device_id=at(k + 1),
            device_id_type=MESH,
        )

    for k in range(3):
        flag_copy(k).start()

    @pl.when(is_first)
    def _():
        loop(PIECES, lambda s: p_down(s).start())
        loop(PIECES, lambda s: first_own(s).start())

    @pl.when(is_second)
    def _():
        loop(PIECES, lambda s: q_up(s).start())
        loop(PIECES, lambda s: p_down(s).start())
        loop(PIECES, lambda s: second_own(s).start())

    load_q = pltpu.make_async_copy(q_hbm, own.at[0], load_sem.at[0])
    load_p = pltpu.make_async_copy(p_hbm, own.at[1], load_sem.at[1])
    load_q.start()
    load_p.start()

    pos = pos_ref[...].astype(jnp.float32)
    upright[...] = jnp.transpose(jnp.broadcast_to(pos, (128, block)))
    top[...] = jnp.full(top.shape, NEG, jnp.float32)
    mass[...] = jnp.zeros(mass.shape, jnp.float32)

    @pl.when(is_first)
    def _():
        line = lax.broadcasted_iota(jnp.int32, (8, block), 0)
        stat_in[0] = jnp.where(line < 4, NEG, 0.0)

    load_q.wait()
    load_p.wait()

    def dot_t(a, b):
        return lax.dot_general(a, b, (((1,), (1,)), ((), ())), preferred_element_type=jnp.float32)

    def fold(side, part):
        before = top[side]
        now = jnp.maximum(before, part)
        mass[side] = mass[side] * jnp.exp(before - now) + jnp.exp(part - now)
        top[side] = now

    def tile(index, start, size):
        per = acc.shape[3] // block
        first = lax.rem(index, per) * block + start
        return (0, index // per, slice(None), pl.ds(pl.multiple_of(first, 128), size))

    def keep(side, index, part, s):
        acc[tile(index, s * rows, rows)] = part
        fold(side, part)

    def diagonal(t):
        side, s = t // PIECES, lax.rem(t, PIECES)
        keep(side, side * 3, dot_t(own[side], own[1 - side, piece(s), :]) * factor, s)

    loop(2 * PIECES, diagonal)
    down = lax.broadcasted_iota(jnp.int32, (block, block), 0).astype(jnp.float32)
    across = lax.broadcasted_iota(jnp.int32, (block, block), 1).astype(jnp.float32)
    row_hit = jnp.sum(jnp.where(pos == down, acc[tile(3, 0, block)], 0.0), axis=0, keepdims=True)
    hit[0] = jnp.broadcast_to(row_hit, (8, block))
    col_hit = jnp.sum(
        jnp.where(upright[:, 0:1] == across, acc[tile(0, 0, block)], 0.0), axis=0, keepdims=True
    )
    hit[1] = jnp.broadcast_to(col_hit, (8, block))
    for k in range(3):
        flag_copy(k).wait_recv()

    def live(side, part, k):
        flag = (flag_out if side == 0 else flag_in)[k - 1, 0:1, 0:1]
        return jnp.where(flag > 0, part, NEG)

    def scores(side, slot, k, start, size):
        lines = pl.ds(pl.multiple_of(start, 128), size)
        return live(side, dot_t(own[side], far[slot, lines, :]) * factor, k)

    def score_piece(side, slot, k, index, s):
        part = scores(side, slot, k, s * rows, rows)
        keep(side, index, part, s)
        return part

    def tell_stats(index, part, s):
        largest = jnp.max(part, axis=0, keepdims=True)
        total = jnp.sum(jnp.exp(part - largest), axis=0, keepdims=True)
        line = lax.broadcasted_iota(jnp.int32, (8, rows), 0)
        stat_out[index, :, piece(s)] = jnp.where(line < 4, largest, total)

    def stat_copy(index, slot, offset):
        return pltpu.make_async_remote_copy(
            src_ref=stat_out.at[index],
            dst_ref=stat_in.at[slot],
            send_sem=stat_send_sem.at[index],
            recv_sem=stat_recv_sem.at[slot],
            device_id=at(offset),
            device_id_type=MESH,
        )

    stat_copies = (stat_copy(0, 1, 2), stat_copy(1, 1, 3), stat_copy(2, 0, -3))

    @pl.when(is_first)
    def _():
        def early(s):
            arrived(0, s)
            score_piece(0, 0, 1, 1, s)

        def soon(s):
            arrived(3, s)
            score_piece(1, 3, 1, 4, s)

        loop(PIECES, early)
        loop(PIECES, soon)

    @pl.when(is_second)
    def _():
        def early(s):
            arrived(3, s)
            score_piece(1, 3, 1, 4, s)

        def soon(s):
            arrived(4, s)
            q_on(s).start()
            second_on(s).start()
            score_piece(1, 4, 2, 5, s)

        loop(PIECES, early)
        loop(PIECES, soon)
        loop(PIECES, lambda s: q_pass(s).start())

    def near(s):
        arrived(1, s)

        @pl.when(is_first)
        def _():
            first_on(s).start()

        @pl.when(is_second)
        def _():
            p_on(s).start()

        part = score_piece(0, 1, 2, 2, s)

        @pl.when(is_first)
        def _():
            tell_stats(0, part, s)
            arrived(2, s)
            tell_stats(1, score_piece(0, 2, 3, 6, s), s)

            @pl.when(s == PIECES - 1)
            def _():
                stat_copies[0].start()
                stat_copies[1].start()

            arrived(5, s)
            tell_stats(2, score_piece(1, 5, 3, 5, s), s)

        @pl.when(is_second)
        def _():
            arrived(0, s)
            p_pass(s).start()
            score_piece(0, 0, 1, 1, s)

    loop(PIECES, near)

    @pl.when(is_first)
    def _():
        stat_copies[2].start()

    @pl.when(is_second)
    def _():
        stat_copies[2].wait_recv()

    stat_copies[0].wait_recv()

    def tell(index, src, dst, offset):
        return pltpu.make_async_remote_copy(
            src_ref=src,
            dst_ref=extra if dst is None else heard.at[dst],
            send_sem=said_sem.at[index],
            recv_sem=heard_sem.at[6 if dst is None else dst],
            device_id=at(offset),
            device_id_type=MESH,
        )

    def first_tells(side):
        sign = 1 if side == 0 else -1
        return [
            tell(side * 3 + k - 1, said.at[side], (1 - side) * 3 + k - 1, sign * k)
            for k in (1, 2, 3)
        ]

    def passed_tells():
        up = [tell(6 + k, extra, 3 + k, 2 + k) for k in range(3)]
        return up + [tell(8 + k, heard.at[0], k, -k) for k in (1, 2)]

    def second_tells(side):
        return [tell(side, said.at[side], None if side == 0 else 0, -1)]

    for side in range(2):
        tops = jnp.transpose(top[side])
        largest = jnp.max(tops, axis=0, keepdims=True)
        total = jnp.sum(
            jnp.transpose(mass[side]) * jnp.exp(tops - largest), axis=0, keepdims=True
        )
        other = stat_in[side, 0:1, :]
        both = jnp.maximum(largest, other)
        total = total * jnp.exp(largest - both) + stat_in[side, 4:5, :] * jnp.exp(other - both)
        value = both + jnp.log(total)
        said[side] = jnp.broadcast_to(value, (8, block))

        @pl.when(is_first)
        def _():
            for copy in first_tells(side):
                copy.start()

        @pl.when(is_second)
        def _():
            for copy in second_tells(side):
                copy.start()

        lse[side] = jnp.transpose(jnp.broadcast_to(value, (128, block)))

    row_ref[...] = said[0, 0:1, :] - hit[0, 0:1, :]
    col_ref[...] = said[1, 0:1, :] - hit[1, 0:1, :]

    strips = block // STRIP

    def strip(i):
        return pl.ds(pl.multiple_of(i * STRIP, STRIP), STRIP)

    def weigh(side, index, theirs, i):
        per = acc.shape[3] // block
        at_tile = side * 3 + index if index < 3 else 6
        lanes = pl.ds(at_tile % per * block, block)
        score = acc[0, at_tile // per, strip(i), lanes]
        value = jnp.exp(score - lse[side, strip(i), 0:1]) + jnp.exp(score - theirs)
        if index == 0:
            if side == 0:
                across = lax.broadcasted_iota(jnp.int32, (STRIP, block), 1)
                match = upright[strip(i), 0:1] == across.astype(jnp.float32)
            else:
                lines = lax.broadcasted_iota(jnp.int32, (STRIP, block), 0) + i * STRIP
                match = pos_ref[...] == lines
            value = value - jnp.where(match, 2.0, 0.0)
        weight[at_tile, strip(i), :] = value.astype(jnp.bfloat16)

    def weigh_diagonal(i):
        for side in range(2):
            weigh(side, 0, said[1 - side, 0:1, :], i)

    def told(dst):
        tell(0, said.at[0], dst, 1).wait_recv()

    told(0)

    @pl.when(is_first)
    def _():
        told(None)
        for copy in passed_tells():
            copy.start()

    loop(strips, weigh_diagonal)
    for dst in range(1, 6):
        told(dst)

    def weigh_far(i):
        weigh(0, 1, heard[0, 0:1, :], i)
        weigh(0, 2, heard[1, 0:1, :], i)
        weigh(1, 1, heard[3, 0:1, :], i)
        weigh(1, 2, heard[5 - second, 0:1, :], i)

    loop(strips, weigh_far)

    @pl.when(is_first)
    def _():
        loop(strips, lambda i: weigh(0, 3, heard[2, 0:1, :], i))

    width = acc.shape[3]
    parts = depth // width

    def columns(j):
        return pl.ds(pl.multiple_of(j * width, width), width)

    def early_grads(side):
        def early_grad(j):
            slots = (0, 1) if side == 0 else (3, 5 - second)
            total = jnp.dot(
                weight[side * 3], own[1 - side, :, columns(j)], preferred_element_type=jnp.float32
            )
            for index, slot in enumerate(slots):
                total += jnp.dot(
                    weight[side * 3 + 1 + index],
                    far[slot, :, columns(j)],
                    preferred_element_type=jnp.float32,
                )
            acc[side, j] = total

        loop(parts, early_grad)

    def weigh_late(side, start, size):
        slot = late[side]
        k = 3 if side == 0 else 2 + second
        part = scores(side, slot, k, start, size)
        theirs = heard[slot, 0:1, pl.ds(start, size)]
        value = jnp.exp(part - lse[side, :, 0:1]) + jnp.exp(part - theirs)
        weight[6 + side, :, pl.ds(start, size)] = value.astype(jnp.bfloat16)

    half = block // 2

    def late_dot(side, start, j):
        return jnp.dot(
            weight[6 + side, :, start : start + half],
            far[late[side], start : start + half, columns(j)],
            preferred_element_type=jnp.float32,
        )

    def begin(side):
        def first_half(j):
            acc[side, j] += late_dot(side, 0, j)

        loop(parts, first_half)

    def finish(side):
        def late_grad(j):
            total = acc[side, j] + late_dot(side, half, j)

            out = dq_ref if side == 0 else dp_ref
            out[:, columns(j)] = (total * factor).astype(jnp.bfloat16)

        loop(parts, late_grad)

    def forward(s):
        @pl.when(is_first)
        def _():
            arrived(4, s)
            q_on(s).start()

    forward(0)
    early_grads(1)
    forward(1)
    early_grads(0)
    forward(2)

    @pl.when(is_first)
    def _():
        begin(0)
        finish(0)

    def late_pieces(side, first, count):
        if side == 1:
            for s in range(first, first + count):
                if s == PIECES - 1:
                    forward(s)

        @pl.when(is_second)
        def _():
            for s in range(first, first + count):
                arrived(2 if side == 0 else 5, s)
            if side == 0:
                weigh_late(0, first * rows, count * rows)

        if side == 1:
            weigh_late(1, first * rows, count * rows)

    late_pieces(0, 0, PIECES // 2)
    late_pieces(1, 0, PIECES // 2)

    @pl.when(is_second)
    def _():
        begin(0)

    begin(1)
    def last_piece(t):
        side, s = lax.rem(t, 2), PIECES // 2 + t // 2

        @pl.when(t == PIECES - 1)
        def _():
            forward(PIECES - 1)

            @pl.when(is_second)
            def _():
                finish(0)

        @pl.when(is_second)
        def _():
            arrived(2 + 3 * side, s)

        @pl.when(is_second | (side == 1))
        def _():
            slot = 2 + side * (2 + second)
            k = 3 - side * (1 - second)
            part = dot_t(own[side], far[slot, piece(s), :]) * factor
            flag = jnp.where(side == 0, flag_out[k - 1, 0:1, :], flag_in[k - 1, 0:1, :])[:, 0:1]
            part = jnp.where(flag > 0, part, NEG)
            theirs = heard[slot, 0:1, piece(s)]
            value = jnp.exp(part - lse[side, :, 0:1]) + jnp.exp(part - theirs)
            weight[6 + side, :, piece(s)] = value.astype(jnp.bfloat16)

    loop(PIECES, last_piece)
    finish(1)

    for k in range(3):
        flag_copy(k).wait_send()
    for copy in (p_down, q_on):
        loop(PIECES, lambda s: copy(s).wait_send())

    @pl.when(is_first)
    def _():
        for copy in (first_own, first_on):
            loop(PIECES, lambda s: copy(s).wait_send())
        for copy in stat_copies + tuple(first_tells(0) + first_tells(1) + passed_tells()):
            copy.wait_send()

    @pl.when(is_second)
    def _():
        for copy in (q_up, p_on, second_own, second_on, p_pass, q_pass):
            loop(PIECES, lambda s: copy(s).wait_send())
        for copy in second_tells(0) + second_tells(1):
            copy.wait_send()


def local(n, queries, passages, links, positives):
    block, depth = queries.shape
    width = min(2 * block, depth // 2)
    flops = 16 * 2 * block * block * depth
    query_grad, passage_grad, row_loss, col_loss = pl.pallas_call(
        functools.partial(kernel, n),
        out_shape=(
            pltpu.VMEM((block, depth), jnp.bfloat16),
            pltpu.VMEM((block, depth), jnp.bfloat16),
            pltpu.VMEM((1, block), jnp.float32),
            pltpu.VMEM((1, block), jnp.float32),
        ),
        in_specs=[
            pl.BlockSpec(memory_space=pl.ANY),
            pl.BlockSpec(memory_space=pl.ANY),
            pl.BlockSpec(memory_space=pltpu.SMEM),
            pl.BlockSpec(memory_space=pltpu.VMEM),
        ],
        out_specs=(
            pl.BlockSpec(memory_space=pltpu.VMEM),
            pl.BlockSpec(memory_space=pltpu.VMEM),
            pl.BlockSpec(memory_space=pltpu.VMEM),
            pl.BlockSpec(memory_space=pltpu.VMEM),
        ),
        scratch_shapes=[
            pltpu.VMEM((2, block, depth), jnp.bfloat16),
            pltpu.VMEM((6, block, depth), jnp.bfloat16),
            pltpu.VMEM((2, max(depth // width, -(-7 * block // width)), block, width), jnp.float32),
            pltpu.VMEM((8, block, block), jnp.bfloat16),
            pltpu.VMEM((2, block, 128), jnp.float32),
            pltpu.VMEM((2, block, 128), jnp.float32),
            pltpu.VMEM((2, block, 128), jnp.float32),
            pltpu.VMEM((block, 128), jnp.float32),
            pltpu.VMEM((2, 8, block), jnp.float32),
            pltpu.VMEM((2, 8, block), jnp.float32),
            pltpu.VMEM((6, 8, block), jnp.float32),
            pltpu.VMEM((8, block), jnp.float32),
            pltpu.VMEM((3, 8, block), jnp.float32),
            pltpu.VMEM((2, 8, block), jnp.float32),
            pltpu.VMEM((3, 8, 128), jnp.float32),
            pltpu.VMEM((3, 8, 128), jnp.float32),
            pltpu.SemaphoreType.DMA((2,)),
            pltpu.SemaphoreType.DMA((8, PIECES)),
            pltpu.SemaphoreType.DMA((6, PIECES)),
            pltpu.SemaphoreType.DMA((11,)),
            pltpu.SemaphoreType.DMA((7,)),
            pltpu.SemaphoreType.DMA((3,)),
            pltpu.SemaphoreType.DMA((3,)),
            pltpu.SemaphoreType.DMA((3,)),
            pltpu.SemaphoreType.DMA((2,)),
        ],
        cost_estimate=pl.CostEstimate(
            flops=flops, bytes_accessed=8 * block * depth, transcendentals=24 * block * block
        ),
        compiler_params=pltpu.CompilerParams(
            collective_id=0, has_side_effects=True, vmem_limit_bytes=55 * 1024 * 1024
        ),
    )(queries, passages, links, positives)
    return query_grad, passage_grad, row_loss.reshape(block), col_loss.reshape(block)


def solution(mesh):
    placed = (P("dp", None), P("dp", None), P("dp", None), P("dp", None))
    return jax.shard_map(
        functools.partial(local, mesh.size),
        mesh=mesh,
        in_specs=placed,
        out_specs=(P("dp", None), P("dp", None), P("dp"), P("dp")),
        check_vma=False,
    )
```
